256 devices in a mesh: slab: 16 (over z_hi, y, core), chan: 16 (over z_lo, x).
Axes of the slice: x: 4, y: 4, z: 8 (z_hi: 2, z_lo: 4; z = z_hi * 4 + z_lo), core: 2. Of those that a mesh axis runs over, the one named last changes fastest.
Arguments:
- volume_in: bfloat16 [1, 64, 128, 4096], P(None, 'chan', 'slab'), may hold values from -6 to 6
- pre_first: bfloat16 [1, 128, 64, 1024], P(None, 'chan', 'slab'), may hold values from -6 to 6
- pre_second: bfloat16 [1, 256, 32, 256], P(None, 'chan', 'slab'), may hold values from -6 to 6
- kernel_first: bfloat16 [27, 64, 128], replicated, may hold values from -0.3125 to 0.3125
- kernel_second: bfloat16 [27, 128, 256], replicated, may hold values from -0.625 to 0.625
- pool_index: int32 [1, 256, 16, 64], P(None, 'chan', 'slab'), may hold values from 0 to 7
- grad_pooled: bfloat16 [1, 256, 16, 64], P(None, 'chan', 'slab'), may hold values from -6 to 6
Outputs:
- grad_volume: bfloat16 [1, 64, 128, 4096], P(None, 'chan', 'slab')
- weight_first: float32 [27, 64, 128], P(None, 'chan', 'slab')
- weight_second: float32 [27, 128, 256], P(None, 'chan', 'slab')
The draws below stay inside these ranges and needn't reach their ends.
Inputs may be any that keep to these rules, and one draw needn't show every extreme that they name: pool_index numbers the window cell as 4 * depth offset + 2 * row offset + column offset.
All inputs are finite; a program needn't handle non-finite values.
Results may differ from the reference program's by a relative error of at most 0.005.
Values may be sent and summed in bfloat16 or wider, within the bound.
No kernel may reach another device: no remote copies, remote signals or barrier semaphores. Data moves between devices by JAX's collectives and lax.ppermute only.
A program may use at most 128 MiB of HBM per device.

```python
import math
import jax
import jax.numpy as jnp
from jax import lax

C0 = 64
C1 = 128
C2 = 256
SAMPLES = 1
H = 64
NDEP = 128


def plant(entries, stream_key, smallest, top_value):
    dims = entries.shape
    place = [jax.random.randint(jax.random.fold_in(stream_key, axis), (), 0, dims[axis]) for axis in range(len(dims))]
    entries = entries.at[tuple(place)].set(smallest)
    longest = dims.index(max(dims))
    place[longest] = (place[longest] + 1) % dims[longest]
    return entries.at[tuple(place)].set(top_value)


def block_scale(rng, shape, pieces, least, top_value):
    loudness = 1.0
    for position, blocks in pieces:
        draws = jax.random.uniform(jax.random.fold_in(jax.random.fold_in(rng, 6), position), (blocks,), jnp.float32, least / len(pieces), top_value / len(pieces))
        loudness = loudness * jnp.repeat(jnp.exp(draws), shape[position] // blocks).reshape((-1,) + (1,) * (len(shape) - 1 - position))
    return loudness


def normal_values(key, shape, spread, most, pieces=(), kind=jnp.bfloat16):
    array = jax.random.normal(key, shape, jnp.float32) * spread
    if len(pieces) > 0:
        array = block_scale(key, shape, pieces, -0.22, 0.18) * array
    return jnp.clip(array, min=-most, max=most).astype(kind)


def setup_inputs(seed: int = 0) -> dict:
    streams_of = jax.random.split(jax.random.key(seed), 8)
    volume_in = normal_values(streams_of[0], (SAMPLES, C0, NDEP, H * H), 1.0, 6.0, ((1, 16), (2, 16)))
    pre_first = normal_values(streams_of[1], (SAMPLES, C1, NDEP // 2, (H // 2) * (H // 2)), 1.0, 6.0, ((1, 16), (2, 16)))
    pre_second = normal_values(streams_of[2], (SAMPLES, C2, NDEP // 4, (H // 4) * (H // 4)), 1.0, 6.0, ((1, 16), (2, 16)))
    kernel_first = normal_values(streams_of[3], (27, C0, C1), (C1 * 27 // 8) ** -0.5, 0.3125)
    kernel_second = normal_values(streams_of[4], (27, C1, C2), (C2 * 27 // 64) ** -0.5, 0.625)
    pool_index = plant(jax.random.randint(streams_of[5], (SAMPLES, C2, NDEP // 8, (H // 8) * (H // 8)), 0, 8), jax.random.fold_in(streams_of[5], 1), 0, 7).astype(jnp.int32)
    grad_pooled = normal_values(streams_of[6], (SAMPLES, C2, NDEP // 8, (H // 8) * (H // 8)), 1.0, 6.0, ((1, 16), (2, 16)))
    return {"volume_in": volume_in, "pre_first": pre_first, "pre_second": pre_second, "kernel_first": kernel_first, "kernel_second": kernel_second, "pool_index": pool_index, "grad_pooled": grad_pooled}


leaky_slope = 0.2

def alternate(blocks, batch, channels, planes, row_count, col_count):
    stacked = jnp.stack([jnp.stack([jnp.stack(inner_list, 0) for inner_list in middle], 0) for middle in blocks], 0)
    moved = jnp.transpose(stacked, (3, 4, 5, 0, 6, 1, 7, 2))
    return moved.reshape(batch, channels, 2 * planes, 2 * row_count, 2 * col_count)

def slope_of(values):
    return jnp.where(values > 0, 1.0, leaky_slope).astype(jnp.float32)

def conv_pullback(activation, kernel, cotangent):
    in_chan = kernel.shape[1]
    out_chan = kernel.shape[2]
    act_wide = activation.astype(jnp.float32)
    kern_wide = kernel.astype(jnp.float32).reshape(3, 3, 3, in_chan, out_chan)

    def forward(act_value, kern_value):
        return lax.conv_general_dilated(act_value, kern_value, (2, 2, 2), [(1, 1), (1, 1), (1, 1)], dimension_numbers=('NCDHW', 'DHWIO', 'NCDHW'), precision=lax.Precision.HIGHEST)
    output, pullback = jax.vjp(forward, act_wide, kern_wide)
    grad_in, grad_kern = pullback(cotangent.astype(jnp.float32))
    return (grad_in, grad_kern.reshape(27, in_chan, out_chan))

def reference(volume_in, pre_first, pre_second, kernel_first, kernel_second, pool_index, grad_pooled):
    half = H // 2
    quarter = H // 4
    eighth = H // 8
    volume = volume_in.reshape(SAMPLES, C0, NDEP, H, H)
    first_pre = pre_first.reshape(SAMPLES, C1, NDEP // 2, half, half).astype(jnp.float32)
    second_pre = pre_second.reshape(SAMPLES, C2, NDEP // 4, quarter, quarter).astype(jnp.float32)
    pooled = grad_pooled.reshape(SAMPLES, C2, NDEP // 8, eighth, eighth).astype(jnp.float32)
    index_cube = pool_index.reshape(SAMPLES, C2, NDEP // 8, eighth, eighth)
    blocks = [[[jnp.where(index_cube == 4 * depth_off + 2 * row_off + col_off, pooled, 0.0).astype(jnp.float32) for col_off in range(2)] for row_off in range(2)] for depth_off in range(2)]
    unpooled = alternate(blocks, SAMPLES, C2, NDEP // 8, eighth, eighth)
    grad_second = (unpooled * slope_of(second_pre)).astype(jnp.bfloat16)
    act_first = jnp.where(first_pre > 0, first_pre, leaky_slope * first_pre).astype(jnp.bfloat16)
    grad_act, taps_second = conv_pullback(act_first, kernel_second, grad_second)
    grad_first = (grad_act * slope_of(first_pre)).astype(jnp.bfloat16)
    grad_in, taps_first = conv_pullback(volume, kernel_first, grad_first)
    grad_volume = grad_in.astype(jnp.bfloat16).reshape(SAMPLES, C0, NDEP, H * H)
    count = SAMPLES * NDEP * H * H
    weight_first = taps_first * (1.0 / math.sqrt(count / 8))
    weight_second = taps_second * (1.0 / math.sqrt(count / 512))
    return (grad_volume, weight_first, weight_second)
```

```python
import math

import jax
import jax.numpy as jnp
import ml_dtypes
import numpy as np
from jax import lax
from jax.experimental import pallas as pl
from jax.experimental.pallas import tpu as pltpu
from jax.sharding import PartitionSpec as P

H = 64
leaky_slope = 0.2
bf16 = jnp.bfloat16
f32 = jnp.float32
variants = ((0, 0), (0, 1), (1, 0), (1, 1))
phase_taps = (((1, 0),), ((2, 0), (0, 1)))


def constant(array):
    return array.astype(ml_dtypes.bfloat16)


def interleave_matrix(width):
    lane = np.arange(512)
    row, col = (lane // width, lane % width)
    source = ((row % 2) * 2 + col % 2) * 128 + (row // 2) * (width // 2) + col // 2
    matrix = np.zeros((512, 512), np.float32)
    matrix[source, lane] = 1
    return matrix


def spread_matrices():
    lane = np.arange(256)
    result = np.zeros((4, 128, 512), np.float32)
    for v, (row_off, col_off) in enumerate(variants):
        row, col = (lane // 16 + row_off, lane % 16 + col_off)
        valid = (row < 16) & (col < 16)
        window = (row // 2) * 8 + col // 2
        result[v, window[valid], lane[valid]] = 1
        result[v, 64 + window[valid], 256 + lane[valid]] = 1
    return result


def row_order():
    matrix = np.zeros((256, 256), np.float32)
    for pair in range(4):
        for group in range(8):
            for parity in range(2):
                for channel in range(4):
                    matrix[
                        ((pair * 8 + group) * 2 + parity) * 4 + channel,
                        (group * 4 + channel) * 8 + 2 * pair + parity,
                    ] = 1
    return matrix


def second_select():
    result = np.zeros((4, 128, 256), np.float32)
    for v, (row_off, col_off) in enumerate(variants):
        for phase in range(4):
            row_phase, col_phase = (phase // 2, phase % 2)
            if row_off > row_phase or col_off > col_phase:
                continue
            row_tap = 0 if row_off else 1 + row_phase
            col_tap = 0 if col_off else 1 + col_phase
            for channel in range(8):
                for start, depth_tap in ((0, 1), (32, 2), (64, 0)):
                    tap = 9 * depth_tap + 3 * row_tap + col_tap
                    result[v, start + phase * 8 + channel, tap * 8 + channel] = 1
    return result


def first_select():
    result = np.zeros((2, 128, 128), np.float32)
    for tap in range(9):
        for channel in range(4):
            result[0, tap * 8 + channel, (9 + tap) * 4 + channel] = 1
            result[0, tap * 8 + 4 + channel, (18 + tap) * 4 + channel] = 1
            result[1, tap * 8 + 4 + channel, tap * 4 + channel] = 1
    return result


def dot(left, right):
    return jnp.dot(left, right, preferred_element_type=f32)


def dot_lanes(left, right):
    return lax.dot_general(left, right, (((1,), (1,)), ((), ())), preferred_element_type=f32)


def slope_of(values):
    return jnp.where(values > 0, 1.0, leaky_slope).astype(f32)


def cell_of(shape, row_off, col_off):
    lane = lax.broadcasted_iota(jnp.int32, shape, 1)
    cell = (((lane >> 4) + row_off) & 1) * 2 + ((lane + col_off) & 1)
    return cell.astype(f32)


def pool_body(pre_ref, index_ref, grad_ref, spread_ref, back_ref, tag_ref, out_ref):
    index = index_ref[...].astype(f32).astype(bf16)
    grad = dot(grad_ref[...], spread_ref[...])
    place = dot(index, spread_ref[...])
    cell = cell_of((16, 256), 0, 0)
    total = jnp.zeros((16, 256), f32)
    for depth in range(2):
        pre = pre_ref[:, depth * 256 : (depth + 1) * 256].astype(f32)
        total = total + jnp.where(place == cell + 4.0 * depth, grad * slope_of(pre), 0.0)
    out_ref[...] = (dot(total.astype(bf16), back_ref[...]) + dot(index, tag_ref[...])).astype(bf16)


def local_body(
    pre_ref, vol_ref, kern_ref, split_one_ref, split_zero_ref, rows_ref,
    act_ref, act_up_ref, cols_ref, kern_out_ref, act_buf, phase_buf, cols_buf, kern_buf,
):
    pre = pre_ref[...].astype(f32)
    act = jnp.where(pre > 0, pre, leaky_slope * pre)
    stacked = jnp.concatenate([act[:, q * 512 : (q + 1) * 512] for q in range(8)], 0)
    split = dot(stacked.astype(bf16), split_one_ref[...])
    act_buf[...] = jnp.zeros_like(act_buf)
    for q in range(8):
        plane, half = (q // 2, q % 2)
        pair, parity = (plane // 2, plane % 2)
        for phase in range(4):
            row = (parity * 4 + phase) * 8
            lane = pair * 256 + half * 128
            piece = split[q * 8 : (q + 1) * 8, phase * 128 : (phase + 1) * 128]
            act_buf[row : row + 8, lane : lane + 128] = piece
            if parity == 1:
                row = 128 + 64 + phase * 8
                act_buf[row : row + 8, lane : lane + 128] = piece
    act_ref[...] = act_buf[0:128, :].astype(bf16)
    act_up_ref[...] = act_buf[128:256, :].astype(bf16)

    wide = jnp.concatenate([vol_ref[:, g * 512 : (g + 1) * 512] for g in range(8)], 0)
    split = dot(wide, split_zero_ref[...]).astype(bf16)
    ordered = dot(rows_ref[...], split)
    for t in range(32):
        for phase in range(4):
            phase_buf[phase * 8 : phase * 8 + 8, t * 128 : (t + 1) * 128] = ordered[
                t * 8 : t * 8 + 8, phase * 128 : (phase + 1) * 128
            ]
    lane = lax.broadcasted_iota(jnp.int32, (8, 4096), 1)
    has_col = (lane & 31) > 0
    has_row = ((lane >> 5) & 31) > 0
    cols_buf[...] = jnp.zeros_like(cols_buf)
    for row_tap in range(3):
        row_phase = 0 if row_tap == 1 else 1
        for col_tap in range(3):
            col_phase = 0 if col_tap == 1 else 1
            phase = row_phase * 2 + col_phase
            value = phase_buf[phase * 8 : phase * 8 + 8, :]
            if col_tap == 0:
                value = jnp.where(has_col, pltpu.roll(value, 1, 1), 0.0)
            if row_tap == 0:
                value = jnp.where(has_row, pltpu.roll(value, 32, 1), 0.0)
            at = (row_tap * 3 + col_tap) * 8
            cols_buf[at : at + 8, :] = value
    cols_ref[...] = cols_buf[...].astype(bf16)

    kern_buf[...] = jnp.zeros_like(kern_buf)
    for tap in range(9):
        kern_buf[tap * 8 : tap * 8 + 4, 0:128] = kern_ref[9 + tap].astype(f32)
        kern_buf[tap * 8 + 4 : tap * 8 + 8, 0:128] = kern_ref[18 + tap].astype(f32)
        kern_buf[tap * 8 + 4 : tap * 8 + 8, 128:256] = kern_ref[tap].astype(f32)
    kern_out_ref[...] = kern_buf[...].astype(bf16)


def channel_block(col_step, row_step):
    me = lax.axis_index("chan")
    return (((me >> 2) + row_step) & 3) * 4 + (((me & 3) + col_step) & 3)


def second_body(
    s0_ref, s1_ref, s2_ref, s3_ref, kern_ref, act_ref, act_up_ref, spread_ref, inter_ref, select_ref,
    grad_ref, taps_ref, small, grid, high, low,
):
    for col_step, ref in enumerate((s0_ref, s1_ref, s2_ref, s3_ref)):
        for row_step in range(4):
            at = pl.multiple_of(channel_block(col_step, row_step) * 16, 16)
            for part in range(2):
                start = (row_step * 2 + part) * 16
                small[part, pl.ds(at, 16), :] = ref[start : start + 16, :]
    both = jnp.concatenate([small[0], small[1]], 0)
    taps = jnp.zeros((256, 256), f32)
    for v, (row_off, col_off) in enumerate(variants):
        wide = dot(both, spread_ref[v])
        cell = cell_of((256, 256), row_off, col_off)
        for plane in range(3):
            base = 256 if plane == 2 else 0
            match = wide[base : base + 256, 256:512] == cell + (4.0 if plane == 1 else 0.0)
            grid[v, :, plane * 256 : (plane + 1) * 256] = jnp.where(
                match, wide[base : base + 256, 0:256], 0.0
            ).astype(bf16)
    for v in range(4):
        part = dot_lanes(grid[v, :, 0:512], act_ref[...])
        part = part + dot_lanes(grid[v, :, 256:768], act_up_ref[...])
        taps = taps + dot(part.astype(bf16), select_ref[v])
    taps_ref[...] = taps.astype(bf16)
    for depth_phase in range(2):
        planes = 3 - depth_phase
        for row_phase in range(2):
            for col_phase in range(2):
                total = jnp.zeros((128, planes * 256), f32)
                for depth_tap, depth_off in phase_taps[depth_phase]:
                    for row_tap, row_off in phase_taps[row_phase]:
                        for col_tap, col_off in phase_taps[col_phase]:
                            total = total + dot(
                                kern_ref[9 * depth_tap + 3 * row_tap + col_tap],
                                grid[
                                    row_off * 2 + col_off,
                                    :,
                                    depth_off * 256 : (depth_off + planes) * 256,
                                ],
                            )
                phase = row_phase * 2 + col_phase
                for pair in range(planes):
                    for half in range(2):
                        q = (2 * pair + depth_phase) * 2 + half
                        lane = pair * 256 + half * 128
                        piece = total[:, lane : lane + 128]
                        rounded = piece.astype(bf16)
                        high[q * 128 : (q + 1) * 128, phase * 128 : (phase + 1) * 128] = rounded
                        low[q * 128 : (q + 1) * 128, phase * 128 : (phase + 1) * 128] = (
                            piece - rounded.astype(f32)
                        ).astype(bf16)
    for q in range(10):
        rows = slice(q * 128, (q + 1) * 128)
        grad_ref[:, q * 512 : (q + 1) * 512] = dot(high[rows, :], inter_ref[...]) + dot(
            low[rows, :], inter_ref[...]
        )


def first_taps_body(
    p0_ref, p1_ref, p2_ref, p3_ref, grad_ref, cols_ref, second_ref, select_ref, first_ref, taps_ref, buf
):
    for col_step, ref in enumerate((p0_ref, p1_ref, p2_ref, p3_ref)):
        slope = slope_of(ref[...].astype(f32))
        for row_step in range(4):
            at = pl.multiple_of(channel_block(col_step, row_step) * 8, 8)
            buf[pl.ds(at, 8), :] = (
                grad_ref[pl.ds(at, 8), :] * slope[row_step * 8 : (row_step + 1) * 8, :]
            )
    grad = buf[...].astype(bf16)
    first_ref[0:128, :] = grad[:, 0:4096]
    first_ref[128:256, :] = grad[:, 1024:5120]
    taps = dot_lanes(first_ref[...], cols_ref[...]).astype(bf16)
    taps = dot(taps[0:128], select_ref[0]) + dot(taps[128:256], select_ref[1])
    for slab in range(16):
        taps_ref[slab, :, 0:256] = second_ref[slab * 16 : (slab + 1) * 16, :]
        taps_ref[slab, :, 256:384] = jnp.concatenate(
            [taps[slab * 8 : (slab + 1) * 8], jnp.zeros((8, 128), f32)], 0
        ).astype(bf16)


def first_body(first_ref, kern_ref, rows_ref, inter_ref, out_ref, buf):
    wide = dot(kern_ref[...], first_ref[...])
    lane = lax.broadcasted_iota(jnp.int32, (8, 4096), 1)
    has_col = (lane & 31) < 31
    has_row = ((lane >> 5) & 31) < 31

    def group(row_tap, col_tap):
        at = (row_tap * 3 + col_tap) * 8
        return wide[at : at + 8, :]

    def next_col(value):
        return jnp.where(has_col, pltpu.roll(value, 4095, 1), 0.0)

    def next_row(value):
        return jnp.where(has_row, pltpu.roll(value, 4096 - 32, 1), 0.0)

    phases = (
        group(1, 1),
        group(1, 2) + next_col(group(1, 0)),
        group(2, 1) + next_row(group(0, 1)),
        group(2, 2) + next_col(group(2, 0)) + next_row(group(0, 2) + next_col(group(0, 0))),
    )
    for t in range(32):
        for phase in range(4):
            buf[t * 8 : (t + 1) * 8, phase * 128 : (phase + 1) * 128] = phases[phase][
                :, t * 128 : (t + 1) * 128
            ]
    ordered = dot(rows_ref[...], buf[...].astype(bf16)).astype(bf16)
    natural = dot(ordered, inter_ref[...])
    for g in range(8):
        for channel in range(4):
            at = g * 32 + channel * 8
            out_ref[0, channel, :, g * 512 : (g + 1) * 512] = natural[at : at + 8, :].astype(bf16)


def final_body(total_ref, first_ref, second_ref):
    total = total_ref[...]
    second = jnp.transpose(total[:, 0:256]) * (1.0 / math.sqrt(1024.0))
    for tap in range(27):
        second_ref[tap] = second[tap * 8 : (tap + 1) * 8, :]
    first = jnp.transpose(total[:, 256:384])[:, 0:8] * (1.0 / math.sqrt(65536.0))
    for tap in range(27):
        first_ref[tap] = first[tap * 4 : (tap + 1) * 4, :]


def call(body, out, scratch=(), flops=1000000):
    return pl.pallas_call(
        body,
        out_shape=out,
        scratch_shapes=list(scratch),
        compiler_params=pltpu.CompilerParams(vmem_limit_bytes=48 * 1024 * 1024),
        cost_estimate=pl.CostEstimate(flops=flops, bytes_accessed=1000000, transcendentals=0),
    )


def shape(dims, dtype=bf16):
    return jax.ShapeDtypeStruct(dims, dtype)


def from_ahead_x(value, step):
    return lax.ppermute(
        value, "chan", [((s // 4) * 4 + (s % 4 + step) % 4, s) for s in range(16)]
    )


def from_ahead_z(value, step):
    return lax.ppermute(value, "chan", [((s + 4 * step) % 16, s) for s in range(16)])


def gather_z(value):
    return jnp.concatenate([value] + [from_ahead_z(value, step) for step in (1, 2, 3)], 0)


def gather_x(value):
    return [value] + [from_ahead_x(value, step) for step in (1, 2, 3)]


def from_above(value):
    return lax.ppermute(value, "slab", [(s, s - 1) for s in range(1, 16)])


def reduce_slabs(parts):
    me = lax.axis_index("slab")
    core, y, z = (me & 1, (me >> 1) & 3, me >> 3)
    parts = parts.reshape((2, 4, 2) + parts.shape[1:])

    def pick(value, index, dim):
        return lax.dynamic_index_in_dim(value, index, dim, False)

    def swap(value, mask):
        return lax.ppermute(value.astype(bf16), "slab", [(s, s ^ mask) for s in range(16)])

    kept = pick(parts, core, 2).astype(f32) + swap(pick(parts, 1 - core, 2), 1).astype(f32)
    kept = pick(kept, z, 0) + swap(pick(kept, 1 - z, 0), 8).astype(f32)
    total = pick(kept, y, 0)
    for step in (1, 2, 3):
        sent = pick(kept, (y + step) & 3, 0).astype(bf16)
        pairs = [(s, (s & 9) | ((((s >> 1) + step) & 3) << 1)) for s in range(16)]
        total = total + lax.ppermute(sent, "slab", pairs).astype(f32)
    return total


def on_device(
    volume_in, pre_first, pre_second, kernel_first, kernel_second, pool_index, grad_pooled
):
    inter_one = interleave_matrix(32)
    inter_zero = interleave_matrix(64)
    spread = spread_matrices()
    rows = row_order()
    back = np.zeros((256, 128), np.float32)
    back[:, 0:64] = spread[0, 0:64, 0:256].T
    tag = np.zeros((64, 128), np.float32)
    tag[np.arange(64), 64 + np.arange(64)] = 1

    pre = pre_first.reshape(8, 4096)
    small = call(pool_body, shape((16, 128)))(
        pre_second.reshape(16, 512),
        pool_index.reshape(16, 64),
        grad_pooled.reshape(16, 64),
        constant(spread[0, 0:64, 0:256]),
        constant(back),
        constant(tag),
    )
    small = jnp.concatenate([small, from_above(small)], 0)
    long = jnp.concatenate([pre, from_above(pre[:, 0:1024])], 1)
    small_all = gather_x(gather_z(small))
    long_all = gather_x(gather_z(long))

    own_kernel = lax.dynamic_slice_in_dim(kernel_first, lax.axis_index("chan") * 4, 4, 1)
    act, act_up, cols, kern = call(
        local_body,
        (shape((128, 512)), shape((128, 512)), shape((128, 4096)), shape((72, 256))),
        (
            pltpu.VMEM((256, 512), f32),
            pltpu.VMEM((32, 4096), f32),
            pltpu.VMEM((128, 4096), f32),
            pltpu.VMEM((72, 256), f32),
        ),
    )(
        pre,
        volume_in.reshape(32, 4096),
        own_kernel,
        constant(inter_one.T),
        constant(inter_zero.T),
        constant(rows),
    )
    grad_act, second = call(
        second_body,
        (shape((128, 5120), f32), shape((256, 256))),
        (
            pltpu.VMEM((2, 256, 128), bf16),
            pltpu.VMEM((4, 256, 768), bf16),
            pltpu.VMEM((1280, 512), bf16),
            pltpu.VMEM((1280, 512), bf16),
        ),
    )(
        *small_all,
        kernel_second,
        act,
        act_up,
        constant(spread),
        constant(inter_one),
        constant(second_select()),
    )
    grad_first, parts = call(
        first_taps_body,
        (shape((256, 4096)), shape((16, 16, 384))),
        (pltpu.VMEM((128, 5120), f32),),
    )(*long_all, grad_act, cols, second, constant(first_select()))
    total = reduce_slabs(parts)
    grad_volume = call(first_body, shape((1, 4, 8, 4096)), (pltpu.VMEM((256, 512), f32),))(
        grad_first, kern, constant(rows.T), constant(inter_zero)
    )
    weight_first, weight_second = call(
        final_body, (shape((27, 4, 8), f32), shape((27, 8, 16), f32))
    )(total)
    return (grad_volume, weight_first, weight_second)


def solution(mesh):
    return jax.shard_map(
        on_device,
        mesh=mesh,
        in_specs=(
            P(None, "chan", "slab", None),
            P(None, "chan", "slab", None),
            P(None, "chan", "slab", None),
            P(),
            P(),
            P(None, "chan", "slab", None),
            P(None, "chan", "slab", None),
        ),
        out_specs=(P(None, "chan", "slab", None), P(None, "chan", "slab"), P(None, "chan", "slab")),
        check_vma=False,
    )
```

```python
import math

import jax
import jax.numpy as jnp
from jax import lax
from jax.experimental import pallas as pl
from jax.experimental.pallas import tpu as pltpu
from jax.sharding import PartitionSpec as P

H = 64
leaky_slope = 0.2
bf16 = jnp.bfloat16
f32 = jnp.float32
variants = ((0, 0), (0, 1), (1, 0), (1, 1))
phase_taps = (((1, 0),), ((2, 0), (0, 1)))


def index_of(shape, dim):
    return lax.broadcasted_iota(jnp.int32, shape, dim)


def one_hot(match):
    return jnp.where(match, 1.0, 0.0).astype(bf16)


def interleave_hot(log_width, to_natural):
    natural = index_of((512, 512), 1 if to_natural else 0)
    phased = index_of((512, 512), 0 if to_natural else 1)
    row, col = (natural >> log_width, natural & ((1 << log_width) - 1))
    source = ((row & 1) << 8) | ((col & 1) << 7) | ((row >> 1) << (log_width - 1)) | (col >> 1)
    return one_hot(source == phased)


def spread_hot(row_off, col_off):
    lane = index_of((128, 512), 1)
    row, col = (((lane >> 4) & 15) + row_off, (lane & 15) + col_off)
    window = ((row >> 1) << 3) + (col >> 1) + ((lane >> 8) << 6)
    match = window == index_of((128, 512), 0)
    return one_hot(match & (row < 16) & (col < 16))


def row_hot(to_grouped):
    new = index_of((256, 256), 0 if to_grouped else 1)
    old = index_of((256, 256), 1 if to_grouped else 0)
    source = (((new >> 3) & 7) << 5) | ((new & 3) << 3) | ((new >> 6) << 1) | ((new >> 2) & 1)
    return one_hot(source == old)


def halo_hot():
    new, old = (index_of((64, 32), 0), index_of((64, 32), 1))
    return one_hot((((new >> 3) << 2 | (new & 3)) == old) & ((new & 4) == 4))


def second_hot(row_off, col_off):
    row, lane = (index_of((128, 256), 0), index_of((128, 256), 1))
    group, row_phase, col_phase = (row >> 5, (row >> 4) & 1, (row >> 3) & 1)
    valid = (group < 3) & (row_phase >= row_off) & (col_phase >= col_off)
    depth_tap = jnp.where(group == 2, 0, group + 1)
    row_tap = 0 if row_off else 1 + row_phase
    col_tap = 0 if col_off else 1 + col_phase
    tap = 9 * depth_tap + 3 * row_tap + col_tap
    return one_hot(valid & (lane == ((row & 7) << 5) + tap))


def first_hot():
    row, lane = (index_of((128, 128), 0), index_of((128, 128), 1))
    tap = jnp.where(row < 72, 9 + 9 * ((row >> 2) & 1) + (row >> 3), (row - 72) >> 2)
    return one_hot((row < 108) & (lane == ((row & 3) << 5) + tap))


def dot(left, right):
    return jnp.dot(left, right, preferred_element_type=f32)


def dot_lanes(left, right):
    return lax.dot_general(left, right, (((1,), (1,)), ((), ())), preferred_element_type=f32)


def slope_of(values):
    return jnp.where(values > 0, 1.0, leaky_slope).astype(f32)


def cell_of(shape, row_off, col_off):
    lane = index_of(shape, 1)
    cell = (((lane >> 4) + row_off) & 1) * 2 + ((lane + col_off) & 1)
    return cell.astype(f32)


def plane_of(value, plane):
    return jnp.sum(jnp.where(index_of(value.shape, 1) == plane, value, 0.0), axis=1)


def pool_body(
    pre_hbm, index_hbm, grad_hbm, out_ref, pre_ref, index_ref, grad_ref, sems
):
    copies = [
        pltpu.make_async_copy(source, target, sems.at[i])
        for i, (source, target) in enumerate(
            ((pre_hbm, pre_ref), (index_hbm, index_ref), (grad_hbm, grad_ref))
        )
    ]
    for copy in copies:
        copy.start()
    cell = cell_of((16, 256), 0, 0)
    lane, window = (index_of((64, 256), 1), index_of((64, 256), 0))
    spread = one_hot((((lane >> 5) << 3) | ((lane >> 1) & 7)) == window)
    lane, window = (index_of((256, 128), 0), index_of((256, 128), 1))
    back = one_hot((((lane >> 5) << 3) | ((lane >> 1) & 7)) == window)
    tag = one_hot(index_of((64, 128), 0) + 64 == index_of((64, 128), 1))
    for copy in copies:
        copy.wait()
    index = index_ref[0, :, 0, :].astype(f32).astype(bf16)
    grad = dot(grad_ref[...], spread)
    place = dot(index, spread)
    total = jnp.zeros((16, 256), f32)
    pre_all = pre_ref[0].astype(f32)
    for depth in range(2):
        pre = plane_of(pre_all, depth)
        total = total + jnp.where(place == cell + 4.0 * depth, grad * slope_of(pre), 0.0)
    out_ref[...] = (dot(total.astype(bf16), back) + dot(index, tag)).astype(bf16)


def plane_body(first_ref, out_ref):
    first = first_ref[0].astype(f32)
    for plane in range(4):
        out_ref[:, plane * 1024 : (plane + 1) * 1024] = plane_of(first, plane).astype(bf16)


def table_body(kern_ref, one_ref, zero_ref, spread_ref, second_ref, row_ref, first_ref, kern_out_ref):
    one_ref[...] = interleave_hot(5, True)
    zero_ref[...] = interleave_hot(6, True)
    for v, (row_off, col_off) in enumerate(variants):
        spread_ref[v] = spread_hot(row_off, col_off)
        second_ref[v] = second_hot(row_off, col_off)
    row_ref[...] = row_hot(False)
    first_ref[...] = first_hot()
    kern_out_ref[...] = kern_ref[...]


def tap_rows(phases):
    shape = (8, phases.shape[1])
    lane = index_of(shape, 1)
    has_col = (lane & 31) > 0
    has_row = ((lane >> 5) & 31) > 0
    result = []
    for row_tap in range(3):
        row_phase = 0 if row_tap == 1 else 1
        for col_tap in range(3):
            col_phase = 0 if col_tap == 1 else 1
            phase = row_phase * 2 + col_phase
            value = phases[phase * 8 : phase * 8 + 8, :]
            if col_tap == 0:
                value = jnp.where(has_col, pltpu.roll(value, 1, 1), 0.0)
            if row_tap == 0:
                value = jnp.where(has_row, pltpu.roll(value, 32, 1), 0.0)
            result.append(value)
    return result


def below_rows(halo, out_ref, phase_buf, cols_buf):
    halo = jnp.concatenate([halo[part * 32 : (part + 1) * 32] for part in range(4)], 1)
    halo = dot(halo_hot(), dot(halo.astype(bf16), interleave_hot(6, False)).astype(bf16))
    for t in range(8):
        for phase in range(4):
            phase_buf[phase * 8 : phase * 8 + 8, t * 128 : (t + 1) * 128] = halo[
                t * 8 : t * 8 + 8, phase * 128 : (phase + 1) * 128
            ]
    cols_buf[...] = jnp.zeros_like(cols_buf)
    for tap, value in enumerate(tap_rows(phase_buf)):
        cols_buf[72 + tap * 4 : 76 + tap * 4, :] = value[4:8, :]
    out_ref[...] = cols_buf[...].astype(bf16)


def local_body(
    pre_ref, vol_ref, kern_ref,
    act_ref, act_up_ref, cols_ref, kern_out_ref, top_ref, act_buf, phase_buf, cols_buf, kern_buf, top_buf,
):
    pre = pre_ref[...].astype(f32)
    act = jnp.where(pre > 0, pre, leaky_slope * pre)
    stacked = jnp.concatenate([act[:, q * 512 : (q + 1) * 512] for q in range(8)], 0)
    split = dot(stacked.astype(bf16), interleave_hot(5, False))
    act_buf[...] = jnp.zeros_like(act_buf)
    for q in range(8):
        plane, half = (q // 2, q % 2)
        pair, parity = (plane // 2, plane % 2)
        for phase in range(4):
            row = (parity * 4 + phase) * 8
            lane = pair * 256 + half * 128
            piece = split[q * 8 : (q + 1) * 8, phase * 128 : (phase + 1) * 128]
            act_buf[row : row + 8, lane : lane + 128] = piece
            if parity == 1:
                row = 128 + 64 + phase * 8
                act_buf[row : row + 8, lane : lane + 128] = piece
    act_ref[...] = act_buf[0:128, :].astype(bf16)
    act_up_ref[...] = act_buf[128:256, :].astype(bf16)

    split_zero = interleave_hot(6, False)
    wide = jnp.concatenate([vol_ref[:, g * 512 : (g + 1) * 512] for g in range(8)], 0)
    ordered = dot(row_hot(True), dot(wide, split_zero).astype(bf16))
    for t in range(32):
        for phase in range(4):
            phase_buf[phase * 8 : phase * 8 + 8, t * 128 : (t + 1) * 128] = ordered[
                t * 8 : t * 8 + 8, phase * 128 : (phase + 1) * 128
            ]
    cols_buf[72:128, :] = jnp.zeros((56, 4096), f32)
    for tap, value in enumerate(tap_rows(phase_buf)):
        cols_buf[tap * 8 : tap * 8 + 8, :] = value
        cols_buf[72 + tap * 4 : 76 + tap * 4, 1024:4096] = value[4:8, 0:3072]
    cols_ref[...] = cols_buf[...].astype(bf16)
    top = plane_of(vol_ref[...].astype(f32).reshape(4, 8, 4096), 7)
    for part in range(4):
        for g in range(8):
            lane = (g * 4 + part) * 128
            top_buf[part * 32 + g * 4 : part * 32 + g * 4 + 4, :] = top[:, lane : lane + 128]
    top_ref[...] = top_buf[...].astype(bf16)

    kern_buf[...] = jnp.zeros_like(kern_buf)
    for tap in range(9):
        kern_buf[tap * 8 : tap * 8 + 4, 0:128] = kern_ref[9 + tap].astype(f32)
        kern_buf[tap * 8 + 4 : tap * 8 + 8, 0:128] = kern_ref[18 + tap].astype(f32)
        kern_buf[tap * 8 + 4 : tap * 8 + 8, 128:256] = kern_ref[tap].astype(f32)
    kern_out_ref[...] = kern_buf[...].astype(bf16)


def channel_block(col_step, row_step):
    me = lax.axis_index("chan")
    return (((me >> 2) + row_step) & 3) * 4 + (((me & 3) + col_step) & 3)


def message_body(pre_ref, s0_ref, s1_ref, s2_ref, s3_ref, out_ref):
    out_ref[:, 0:4096] = pre_ref[...]
    for step, ref in enumerate((s0_ref, s1_ref, s2_ref, s3_ref)):
        rows = ref[...].astype(f32)
        for half in range(2):
            lane = 4096 + (step * 2 + half) * 128
            out_ref[:, lane : lane + 128] = rows[half * 8 : half * 8 + 8, :].astype(bf16)


def join_body(m0_ref, m1_ref, m2_ref, m3_ref, after_ref, table_ref, out_ref):
    rows = [ref[:, 0:4096].astype(f32) for ref in (m0_ref, m1_ref, m2_ref, m3_ref)]
    out_ref[...] = jnp.concatenate(rows, 0).astype(bf16)


def order_body(m0_ref, m1_ref, m2_ref, m3_ref, top_ref, out_ref, one_ref, two_ref):
    for row_step, ref in enumerate((m0_ref, m1_ref, m2_ref, m3_ref)):
        for col_step in range(4):
            at = pl.multiple_of(channel_block(col_step, row_step) * 16, 16)
            lane = 4096 + col_step * 256
            rows = [ref[:, lane + half * 128 : lane + half * 128 + 128].astype(f32) for half in range(2)]
            out_ref[pl.ds(at, 16), :] = jnp.concatenate(rows, 0).astype(bf16)
    up = jnp.concatenate([top_ref[...].astype(f32), jnp.zeros((128, 128), f32)], 0)
    down = out_ref[...].astype(f32)
    odd = (lax.axis_index("slab") & 1).astype(f32)
    one_ref[...] = (up + odd * (down - up)).astype(bf16)
    two_ref[...] = (down + odd * (up - down)).astype(bf16)


def second_body(
    small_ref, kern_ref, act_ref, act_up_ref, spread_ref, inter_ref, grad_ref, taps_ref, grid, high, low
):
    small = small_ref[...]
    for v, (row_off, col_off) in enumerate(variants):
        wide = dot(small, spread_ref[v])
        cell = cell_of((256, 256), row_off, col_off)
        for plane in range(2):
            match = wide[:, 256:512] == cell + 4.0 * plane
            grid[v, :, plane * 256 : (plane + 1) * 256] = jnp.where(
                match, wide[:, 0:256], 0.0
            ).astype(bf16)
    for v in range(4):
        taps_ref[v] = dot_lanes(grid[v], act_ref[...]) + dot_lanes(
            grid[v, :, 256:512], act_up_ref[:, 0:256]
        )
    for depth_phase in range(2):
        for row_phase in range(2):
            for col_phase in range(2):
                total = jnp.zeros((128, 512), f32)
                ahead = jnp.zeros((128, 256), f32)
                for row_tap, row_off in phase_taps[row_phase]:
                    for col_tap, col_off in phase_taps[col_phase]:
                        tap = 3 * row_tap + col_tap
                        v = row_off * 2 + col_off
                        total = total + dot(kern_ref[9 + 9 * depth_phase + tap], grid[v])
                        if depth_phase == 1:
                            ahead = ahead + dot(kern_ref[tap], grid[v, :, 256:512])
                phase = row_phase * 2 + col_phase
                for pair in range(2):
                    for half in range(2):
                        q = (2 * pair + depth_phase) * 2 + half
                        lane = pair * 256 + half * 128
                        piece = total[:, lane : lane + 128]
                        if pair == 0 and depth_phase == 1:
                            piece = piece + ahead[:, lane : lane + 128]
                        put_split(high, low, q, phase, piece)
    inter = inter_ref[...]
    for q in range(8):
        rows = slice(q * 128, (q + 1) * 128)
        grad_ref[:, q * 512 : (q + 1) * 512] = dot(high[rows, :], inter) + dot(low[rows, :], inter)


def put_split(high, low, q, phase, piece):
    rounded = piece.astype(bf16)
    high[q * 128 : (q + 1) * 128, phase * 128 : (phase + 1) * 128] = rounded
    low[q * 128 : (q + 1) * 128, phase * 128 : (phase + 1) * 128] = (
        piece - rounded.astype(f32)
    ).astype(bf16)


def second_halo_body(
    one_ref, two_ref, kern_ref, act_up_ref, taps_in_ref, spread_ref, select_ref, inter_ref,
    grad_ref, taps_ref, below_ref, high, low, phase_buf, cols_buf,
):
    one, two = (one_ref[...].astype(f32), two_ref[...].astype(f32))
    odd = (lax.axis_index("slab") & 1).astype(f32)
    above = (one + odd * (two - one)).astype(bf16)
    below_rows((two + odd * (one - two))[0:128], below_ref, phase_buf, cols_buf)
    taps = jnp.zeros((256, 256), f32)
    grid = []
    for v, (row_off, col_off) in enumerate(variants):
        wide = dot(above, spread_ref[v])
        match = wide[:, 256:512] == cell_of((256, 256), row_off, col_off)
        grid.append(jnp.where(match, wide[:, 0:256], 0.0).astype(bf16))
        part = taps_in_ref[v] + dot_lanes(grid[v], act_up_ref[:, 256:512])
        taps = taps + dot(part.astype(bf16), select_ref[v])
    taps_ref[...] = taps.astype(bf16)
    for row_phase in range(2):
        for col_phase in range(2):
            total = jnp.zeros((128, 256), f32)
            for row_tap, row_off in phase_taps[row_phase]:
                for col_tap, col_off in phase_taps[col_phase]:
                    total = total + dot(kern_ref[3 * row_tap + col_tap], grid[row_off * 2 + col_off])
            for half in range(2):
                put_split(high, low, half, row_phase * 2 + col_phase, total[:, half * 128 : half * 128 + 128])
    inter = inter_ref[...]
    for q in range(2):
        rows = slice(q * 128, (q + 1) * 128)
        grad_ref[:, q * 512 : (q + 1) * 512] = dot(high[rows, :], inter) + dot(low[rows, :], inter)


def next_col(value):
    lane = index_of(value.shape, 1)
    return jnp.where((lane & 31) < 31, pltpu.roll(value, value.shape[1] - 1, 1), 0.0)


def next_row(value):
    lane = index_of(value.shape, 1)
    return jnp.where(((lane >> 5) & 31) < 31, pltpu.roll(value, value.shape[1] - 32, 1), 0.0)


def fold_taps(wide):
    def group(row_tap, col_tap):
        at = (row_tap * 3 + col_tap) * 8
        return wide[at : at + 8, :]

    return (
        group(1, 1),
        group(1, 2) + next_col(group(1, 0)),
        group(2, 1) + next_row(group(0, 1)),
        group(2, 2) + next_col(group(2, 0)) + next_row(group(0, 2) + next_col(group(0, 0))),
    )


def first_taps_body(
    p0_ref, p1_ref, p2_ref, p3_ref, grad_ref, halo_ref, cols_ref, below_ref, second_ref, kern_ref, select_ref,
    first_ref, kept_ref, sent_ref, edge_ref, buf, taps_buf,
):
    for col_step, ref in enumerate((p0_ref, p1_ref, p2_ref, p3_ref)):
        slope = slope_of(ref[...].astype(f32))
        for row_step in range(4):
            at = pl.multiple_of(channel_block(col_step, row_step) * 8, 8)
            rows = slope[row_step * 8 : (row_step + 1) * 8, :]
            buf[pl.ds(at, 8), 0:3072] = grad_ref[pl.ds(at, 8), 0:3072] * rows[:, 0:3072]
            last = grad_ref[pl.ds(at, 8), 3072:4096] + halo_ref[pl.ds(at, 8), :]
            buf[pl.ds(at, 8), 3072:4096] = last * rows[:, 3072:4096]
    grad = buf[...].astype(bf16)
    first_ref[0:128, :] = grad
    first_ref[128:256, 0:3072] = grad[:, 1024:4096]
    first_ref[128:256, 3072:4096] = jnp.zeros((128, 1024), bf16)
    taps = dot_lanes(first_ref[0:128, :], cols_ref[...])
    taps = (taps + dot_lanes(first_ref[0:128, 0:1024], below_ref[...])).astype(bf16)
    taps_buf[...] = dot(taps, select_ref[...])
    core = lax.axis_index("slab") & 1
    for pair in range(8):
        for ref, which in ((kept_ref, core), (sent_ref, 1 - core)):
            slab = pair * 2 + which
            ref[pair, :, 0:256] = second_ref[pl.ds(pl.multiple_of(slab * 16, 16), 16), :]
            part = taps_buf[pl.ds(pl.multiple_of(slab * 8, 8), 8), :]
            ref[pair, :, 256:384] = jnp.concatenate([part, jnp.zeros((8, 128), f32)], 0).astype(bf16)
    edges = fold_taps(dot(kern_ref[:, 128:256], first_ref[0:128, 0:1024]))
    edge_ref[...] = jnp.concatenate([edge[4:8, :] for edge in edges], 0).astype(bf16)


def first_body(first_ref, kern_ref, edge_ref, rows_ref, inter_ref, out_ref, buf):
    phases = fold_taps(dot(kern_ref[...], first_ref[...]))
    edge = edge_ref[...].astype(f32)
    for t in range(32):
        for phase in range(4):
            value = phases[phase][:, t * 128 : (t + 1) * 128]
            if t >= 24:
                lane = (t - 24) * 128
                extra = edge[phase * 4 : (phase + 1) * 4, lane : lane + 128]
                value = value + jnp.concatenate([jnp.zeros((4, 128), f32), extra], 0)
            buf[t * 8 : (t + 1) * 8, phase * 128 : (phase + 1) * 128] = value
    ordered = dot(rows_ref[...], buf[...].astype(bf16)).astype(bf16)
    natural = dot(ordered, inter_ref[...])
    for g in range(8):
        for channel in range(4):
            at = g * 32 + channel * 8
            out_ref[0, channel, :, g * 512 : (g + 1) * 512] = natural[at : at + 8, :].astype(bf16)


def middle_body(kept_ref, came_ref, next_ref, s1_ref, s2_ref, s3_ref):
    y = (lax.axis_index("slab") >> 1) & 3
    for z in range(2):
        for step, ref in enumerate((next_ref, s1_ref, s2_ref, s3_ref)):
            at = z * 4 + ((y + step) & 3)
            value = kept_ref[at].astype(f32) + came_ref[at].astype(f32)
            ref[z] = value.astype(ref.dtype)


def late_body(kept_ref, c1_ref, c2_ref, c3_ref, next_ref, sent_ref):
    z = lax.axis_index("slab") >> 3

    def total(at):
        value = kept_ref[at]
        for ref in (c1_ref, c2_ref, c3_ref):
            value = value + ref[at].astype(f32)
        return value

    next_ref[...] = total(z)
    sent_ref[...] = total(1 - z).astype(bf16)


def final_body(kept_ref, came_ref, first_ref, second_ref):
    total = kept_ref[...] + came_ref[...].astype(f32)
    for channel in range(8):
        at = channel * 32
        second_ref[channel] = total[:, at : at + 27] * (1.0 / math.sqrt(1024.0))
    for channel in range(4):
        at = 256 + channel * 32
        first_ref[channel] = total[0:8, at : at + 27] * (1.0 / math.sqrt(65536.0))


def call(body, out, scratch=(), micros=0.05, limit=16, **options):
    return pl.pallas_call(
        body,
        out_shape=out,
        scratch_shapes=list(scratch),
        compiler_params=pltpu.CompilerParams(vmem_limit_bytes=limit * 1024 * 1024),
        cost_estimate=pl.CostEstimate(
            flops=int(micros * 1.0e9), bytes_accessed=100000, transcendentals=0
        ),
        **options,
    )


def shape(dims, dtype=bf16):
    return jax.ShapeDtypeStruct(dims, dtype)


def from_ahead_x(value, step):
    return lax.ppermute(
        value, "chan", [((s // 4) * 4 + (s % 4 + step) % 4, s) for s in range(16)]
    )


def from_ahead_z(value, step):
    return lax.ppermute(value, "chan", [((s + 4 * step) % 16, s) for s in range(16)])


def gather(value, exchange):
    return [value] + [exchange(value, step) for step in (1, 2, 3)]


def from_above(value):
    return lax.ppermute(value, "slab", [(s, s - 1) for s in range(1, 16)])


def swap_next(value):
    pairs = [(s, s + 1) for s in range(1, 14, 2)] + [(s + 1, s) for s in range(1, 14, 2)]
    return lax.ppermute(value, "slab", pairs)


def swap(value, axis, mask):
    return lax.ppermute(value, axis, [(s, s ^ mask) for s in range(16)])


def on_device(
    volume_in, pre_first, pre_second, kernel_first, kernel_second, pool_index, grad_pooled
):
    small = call(
        pool_body,
        shape((16, 128)),
        (
            pltpu.VMEM((1, 16, 2, 256), bf16),
            pltpu.VMEM((1, 16, 1, 64), jnp.int32),
            pltpu.VMEM((16, 64), bf16),
            pltpu.SemaphoreType.DMA((3,)),
        ),
        limit=60,
        in_specs=[pl.BlockSpec(memory_space=pltpu.HBM)] * 3,
    )(pre_second, pool_index, grad_pooled.reshape(16, 64))
    pre = call(plane_body, shape((8, 4096)))(pre_first)

    inter_one, inter_zero, spread, select_second, rows, select_first, kernel_second = call(
        table_body,
        (
            shape((512, 512)),
            shape((512, 512)),
            shape((4, 128, 512)),
            shape((4, 128, 256)),
            shape((256, 256)),
            shape((128, 128)),
            shape((27, 128, 256)),
        ),
    )(kernel_second)
    own_kernel = lax.dynamic_slice_in_dim(kernel_first, lax.axis_index("chan") * 4, 4, 1)
    act, act_up, cols, kern, top = call(
        local_body,
        (shape((128, 512)), shape((128, 512)), shape((128, 4096)), shape((72, 256)), shape((128, 128))),
        (
            pltpu.VMEM((256, 512), f32),
            pltpu.VMEM((32, 4096), f32),
            pltpu.VMEM((128, 4096), f32),
            pltpu.VMEM((72, 256), f32),
            pltpu.VMEM((128, 128), f32),
        ),
    )(pre, volume_in.reshape(32, 4096), own_kernel)

    message = call(message_body, shape((8, 5120)))(pre, *gather(small, from_ahead_x))
    messages = gather(message, from_ahead_z)
    whole = pl.BlockSpec(memory_space=pltpu.VMEM)
    unread = pl.BlockSpec(memory_space=pl.ANY)
    pre_rows = call(join_body, shape((32, 4096)), in_specs=[whole] * 4 + [unread] * 2)(
        *messages, top, select_first
    )
    pre_all = gather(pre_rows, from_ahead_x)
    block = (256, 128)
    small, one, two = call(order_body, (shape(block), shape(block), shape(block)))(*messages, top)
    one, two = (swap(one, "slab", 1), swap_next(two))
    grad_act, second = call(
        second_body,
        (shape((128, 4096), f32), shape((4, 256, 128), f32)),
        (pltpu.VMEM((4, 256, 512), bf16), pltpu.VMEM((1024, 512), bf16), pltpu.VMEM((1024, 512), bf16)),
    )(small, kernel_second, act, act_up, spread, inter_one)
    grad_halo, second, below = call(
        second_halo_body,
        (shape((128, 1024), f32), shape((256, 256)), shape((128, 1024))),
        (
            pltpu.VMEM((256, 512), bf16),
            pltpu.VMEM((256, 512), bf16),
            pltpu.VMEM((32, 1024), f32),
            pltpu.VMEM((128, 1024), f32),
        ),
    )(one, two, kernel_second, act_up, second, spread, select_second, inter_one)
    grad_first, kept, sent, edge = call(
        first_taps_body,
        (shape((256, 4096)), shape((8, 16, 384)), shape((8, 16, 384)), shape((16, 1024))),
        (pltpu.VMEM((128, 4096), f32), pltpu.VMEM((128, 128), f32)),
    )(*pre_all, grad_act, grad_halo, cols, below, second, kern, select_first)

    block = (2, 16, 384)
    kept, *sent = call(
        middle_body, (shape(block, f32), shape(block), shape(block), shape(block))
    )(kept, swap(sent, "slab", 1))
    came = []
    for step in (1, 2, 3):
        pairs = [(s, (s & 9) | ((((s >> 1) + step) & 3) << 1)) for s in range(16)]
        came.append(lax.ppermute(sent[step - 1], "slab", pairs))
    kept, sent = call(late_body, (shape((16, 384), f32), shape((16, 384))))(kept, *came)
    grad_volume = call(first_body, shape((1, 4, 8, 4096)), (pltpu.VMEM((256, 512), f32),))(
        grad_first, kern, from_above(edge), rows, inter_zero
    )
    weight_first, weight_second = call(
        final_body, (shape((4, 8, 27), f32), shape((8, 16, 27), f32))
    )(kept, swap(sent, "slab", 8))
    return (
        grad_volume,
        jnp.transpose(weight_first, (2, 0, 1)),
        jnp.transpose(weight_second, (2, 0, 1)),
    )


def solution(mesh):
    return jax.shard_map(
        on_device,
        mesh=mesh,
        in_specs=(
            P(None, "chan", "slab", None),
            P(None, "chan", "slab", None),
            P(None, "chan", "slab", None),
            P(),
            P(),
            P(None, "chan", "slab", None),
            P(None, "chan", "slab", None),
        ),
        out_specs=(P(None, "chan", "slab", None), P(None, "chan", "slab"), P(None, "chan", "slab")),
        check_vma=False,
    )
```

```python
import math

import jax
import jax.numpy as jnp
from jax import lax
from jax.experimental import pallas as pl
from jax.experimental.pallas import tpu as pltpu
from jax.sharding import PartitionSpec as P

H = 64
leaky_slope = 0.2
bf16 = jnp.bfloat16
f32 = jnp.float32
variants = ((0, 0), (0, 1), (1, 0), (1, 1))
phase_taps = (((1, 0),), ((2, 0), (0, 1)))


def index_of(shape, dim):
    return lax.broadcasted_iota(jnp.int32, shape, dim)


def rows_of(count):
    return index_of((count, 1), 0)


def lanes_of(count):
    return index_of((1, count), 1)


def one_hot(match):
    return jnp.where(match, 1.0, 0.0).astype(bf16)


def interleave_hot(log_width, to_natural):
    natural = lanes_of(512) if to_natural else rows_of(512)
    row, col = (natural >> log_width, natural & ((1 << log_width) - 1))
    source = ((row & 1) << 8) | ((col & 1) << 7) | ((row >> 1) << (log_width - 1)) | (col >> 1)
    return one_hot(source == index_of((512, 512), 0 if to_natural else 1))


def spread_hot(row_off, col_off):
    lane = lanes_of(512)
    row, col = (((lane >> 4) & 15) + row_off, (lane & 15) + col_off)
    window = ((row >> 1) << 3) + (col >> 1) + ((lane >> 8) << 6)
    window = jnp.where((row < 16) & (col < 16), window, -1)
    return one_hot(window == index_of((128, 512), 0))


def row_hot(to_grouped):
    new = rows_of(256) if to_grouped else lanes_of(256)
    source = (((new >> 3) & 7) << 5) | ((new & 3) << 3) | ((new >> 6) << 1) | ((new >> 2) & 1)
    return one_hot(source == index_of((256, 256), 1 if to_grouped else 0))


def halo_hot():
    new, old = (index_of((64, 32), 0), index_of((64, 32), 1))
    return one_hot((((new >> 3) << 2 | (new & 3)) == old) & ((new & 4) == 4))


def second_hot(row_off, col_off):
    row = rows_of(128)
    group, row_phase, col_phase = (row >> 5, (row >> 4) & 1, (row >> 3) & 1)
    depth_tap = jnp.where(group == 2, 0, group + 1)
    row_tap = 0 if row_off else 1 + row_phase
    col_tap = 0 if col_off else 1 + col_phase
    target = ((row & 7) << 5) + 9 * depth_tap + 3 * row_tap + col_tap
    valid = (group < 3) & (row_phase >= row_off) & (col_phase >= col_off)
    return one_hot(jnp.where(valid, target, -1) == index_of((128, 256), 1))


def first_hot():
    row = rows_of(128)
    tap = jnp.where(row < 72, 9 + 9 * ((row >> 2) & 1) + (row >> 3), (row - 72) >> 2)
    target = jnp.where(row < 108, ((row & 3) << 5) + tap, -1)
    return one_hot(target == index_of((128, 128), 1))


def dot(left, right):
    return jnp.dot(left, right, preferred_element_type=f32)


def dot_lanes(left, right):
    return lax.dot_general(left, right, (((1,), (1,)), ((), ())), preferred_element_type=f32)


def slope_of(values):
    return jnp.where(values > 0, 1.0, leaky_slope).astype(f32)


def cell_of(row_off, col_off):
    lane = lanes_of(256)
    cell = (((lane >> 4) + row_off) & 1) * 2 + ((lane + col_off) & 1)
    return cell.astype(f32)


def plane_of(value, plane):
    return jnp.sum(jnp.where(index_of(value.shape, 1) == plane, value, 0.0), axis=1)


def pool_body(
    pre_hbm, index_hbm, grad_hbm, first_hbm, out_ref, pre_ref, index_ref, grad_ref, first_ref, sems
):
    copies = [
        pltpu.make_async_copy(source, target, sems.at[i])
        for i, (source, target) in enumerate(
            ((first_hbm, first_ref), (pre_hbm, pre_ref), (index_hbm, index_ref), (grad_hbm, grad_ref))
        )
    ]
    for copy in copies:
        copy.start()
    cell = cell_of(0, 0)
    lane = lanes_of(256)
    spread = one_hot((((lane >> 5) << 3) | ((lane >> 1) & 7)) == index_of((64, 256), 0))
    lane = rows_of(256)
    back = one_hot((((lane >> 5) << 3) | ((lane >> 1) & 7)) == index_of((256, 128), 1))
    tag = one_hot(rows_of(64) + 64 == index_of((64, 128), 1))
    copies[0].wait()
    first = first_ref[0].astype(f32)
    for plane in range(4):
        out_ref[:, plane * 1024 : (plane + 1) * 1024] = plane_of(first, plane).astype(bf16)
    for copy in copies[1:]:
        copy.wait()
    index = index_ref[0, :, 0, :].astype(f32).astype(bf16)
    grad = dot(grad_ref[...], spread)
    place = dot(index, spread)
    total = jnp.zeros((16, 256), f32)
    pre_all = pre_ref[0].astype(f32)
    for depth in range(2):
        pre = plane_of(pre_all, depth)
        total = total + jnp.where(place == cell + 4.0 * depth, grad * slope_of(pre), 0.0)
    small = dot(total.astype(bf16), back) + dot(index, tag)
    out_ref[:, 4096:4224] = small[0:8].astype(bf16)
    out_ref[:, 4224:4352] = small[8:16].astype(bf16)


def hold_body(kern_ref, out_ref):
    out_ref[...] = kern_ref[...]


def tap_rows(phases):
    lane = lanes_of(phases.shape[1])
    has_col = (lane & 31) > 0
    has_row = ((lane >> 5) & 31) > 0
    result = []
    for row_tap in range(3):
        row_phase = 0 if row_tap == 1 else 1
        for col_tap in range(3):
            col_phase = 0 if col_tap == 1 else 1
            phase = row_phase * 2 + col_phase
            value = phases[phase * 8 : phase * 8 + 8, :]
            if col_tap == 0:
                value = jnp.where(has_col, pltpu.roll(value, 1, 1), 0.0)
            if row_tap == 0:
                value = jnp.where(has_row, pltpu.roll(value, 32, 1), 0.0)
            result.append(value)
    return result


def below_rows(halo, out_ref, phase_buf, cols_buf):
    halo = jnp.concatenate([halo[part * 32 : (part + 1) * 32] for part in range(4)], 1)
    halo = dot(halo_hot(), dot(halo.astype(bf16), interleave_hot(6, False)).astype(bf16))
    for t in range(8):
        for phase in range(4):
            phase_buf[phase * 8 : phase * 8 + 8, t * 128 : (t + 1) * 128] = halo[
                t * 8 : t * 8 + 8, phase * 128 : (phase + 1) * 128
            ]
    cols_buf[...] = jnp.zeros_like(cols_buf)
    for tap, value in enumerate(tap_rows(phase_buf)):
        cols_buf[72 + tap * 4 : 76 + tap * 4, :] = value[4:8, :]
    out_ref[...] = cols_buf[...].astype(bf16)


def local_body(
    pre_ref, vol_ref, kern_ref,
    act_ref, act_up_ref, cols_ref, kern_out_ref, top_ref, act_buf, phase_buf, cols_buf, kern_buf, top_buf,
):
    pre = pre_ref[:, 0:4096].astype(f32)
    act = jnp.where(pre > 0, pre, leaky_slope * pre)
    stacked = jnp.concatenate([act[:, q * 512 : (q + 1) * 512] for q in range(8)], 0)
    split = dot(stacked.astype(bf16), interleave_hot(5, False))
    act_buf[...] = jnp.zeros_like(act_buf)
    for q in range(8):
        plane, half = (q // 2, q % 2)
        pair, parity = (plane // 2, plane % 2)
        for phase in range(4):
            row = (parity * 4 + phase) * 8
            lane = pair * 256 + half * 128
            piece = split[q * 8 : (q + 1) * 8, phase * 128 : (phase + 1) * 128]
            act_buf[row : row + 8, lane : lane + 128] = piece
            if parity == 1:
                row = 128 + 64 + phase * 8
                act_buf[row : row + 8, lane : lane + 128] = piece
    act_ref[...] = act_buf[0:128, :].astype(bf16)
    act_up_ref[...] = act_buf[128:256, :].astype(bf16)

    split_zero = interleave_hot(6, False)
    wide = jnp.concatenate([vol_ref[:, g * 512 : (g + 1) * 512] for g in range(8)], 0)
    ordered = dot(row_hot(True), dot(wide, split_zero).astype(bf16))
    for t in range(32):
        for phase in range(4):
            phase_buf[phase * 8 : phase * 8 + 8, t * 128 : (t + 1) * 128] = ordered[
                t * 8 : t * 8 + 8, phase * 128 : (phase + 1) * 128
            ]
    cols_buf[72:128, :] = jnp.zeros((56, 4096), f32)
    for tap, value in enumerate(tap_rows(phase_buf)):
        cols_buf[tap * 8 : tap * 8 + 8, :] = value
        cols_buf[72 + tap * 4 : 76 + tap * 4, 1024:4096] = value[4:8, 0:3072]
    cols_ref[...] = cols_buf[...].astype(bf16)
    top = plane_of(vol_ref[...].astype(f32).reshape(4, 8, 4096), 7)
    for part in range(4):
        for g in range(8):
            lane = (g * 4 + part) * 128
            top_buf[part * 32 + g * 4 : part * 32 + g * 4 + 4, :] = top[:, lane : lane + 128]
    top_ref[...] = top_buf[...].astype(bf16)

    kern_buf[...] = jnp.zeros_like(kern_buf)
    for tap in range(9):
        kern_buf[tap * 8 : tap * 8 + 4, 0:128] = kern_ref[9 + tap].astype(f32)
        kern_buf[tap * 8 + 4 : tap * 8 + 8, 0:128] = kern_ref[18 + tap].astype(f32)
        kern_buf[tap * 8 + 4 : tap * 8 + 8, 128:256] = kern_ref[tap].astype(f32)
    kern_out_ref[...] = kern_buf[...].astype(bf16)


def channel_block(col_step, row_step):
    me = lax.axis_index("chan")
    return (((me >> 2) + row_step) & 3) * 4 + (((me & 3) + col_step) & 3)


def join_small_body(m0_ref, m1_ref, m2_ref, m3_ref, after_ref, table_ref, out_ref):
    for step, ref in enumerate((m0_ref, m1_ref, m2_ref, m3_ref)):
        rows = jnp.concatenate([ref[:, 4096:4224].astype(f32), ref[:, 4224:4352].astype(f32)], 0)
        out_ref[step * 16 : step * 16 + 16, :] = rows.astype(bf16)


def join_body(m0_ref, m1_ref, m2_ref, m3_ref, out_ref):
    rows = [ref[:, 0:4096].astype(f32) for ref in (m0_ref, m1_ref, m2_ref, m3_ref)]
    out_ref[...] = jnp.concatenate(rows, 0).astype(bf16)


def order_body(s0_ref, s1_ref, s2_ref, s3_ref, top_ref, out_ref, one_ref, two_ref):
    for col_step, ref in enumerate((s0_ref, s1_ref, s2_ref, s3_ref)):
        for row_step in range(4):
            at = pl.multiple_of(channel_block(col_step, row_step) * 16, 16)
            out_ref[pl.ds(at, 16), :] = ref[row_step * 16 : row_step * 16 + 16, :]
    up = jnp.concatenate([top_ref[...].astype(f32), jnp.zeros((128, 128), f32)], 0)
    down = out_ref[...].astype(f32)
    odd = (lax.axis_index("slab") & 1).astype(f32)
    one_ref[...] = (up + odd * (down - up)).astype(bf16)
    two_ref[...] = (down + odd * (up - down)).astype(bf16)


def second_body(
    small_ref, kern_ref, act_ref, act_up_ref, grad_ref, taps_ref, grid, high, low
):
    small = small_ref[...]
    for v, (row_off, col_off) in enumerate(variants):
        wide = dot(small, spread_hot(row_off, col_off))
        cell = cell_of(row_off, col_off)
        for plane in range(2):
            match = wide[:, 256:512] == cell + 4.0 * plane
            grid[v, :, plane * 256 : (plane + 1) * 256] = jnp.where(
                match, wide[:, 0:256], 0.0
            ).astype(bf16)
    for v in range(4):
        taps_ref[v] = dot_lanes(grid[v], act_ref[...]) + dot_lanes(
            grid[v, :, 256:512], act_up_ref[:, 0:256]
        )
    for depth_phase in range(2):
        for row_phase in range(2):
            for col_phase in range(2):
                total = jnp.zeros((128, 512), f32)
                ahead = jnp.zeros((128, 256), f32)
                for row_tap, row_off in phase_taps[row_phase]:
                    for col_tap, col_off in phase_taps[col_phase]:
                        tap = 3 * row_tap + col_tap
                        v = row_off * 2 + col_off
                        total = total + dot(kern_ref[9 + 9 * depth_phase + tap], grid[v])
                        if depth_phase == 1:
                            ahead = ahead + dot(kern_ref[tap], grid[v, :, 256:512])
                phase = row_phase * 2 + col_phase
                for pair in range(2):
                    for half in range(2):
                        q = (2 * pair + depth_phase) * 2 + half
                        lane = pair * 256 + half * 128
                        piece = total[:, lane : lane + 128]
                        if pair == 0 and depth_phase == 1:
                            piece = piece + ahead[:, lane : lane + 128]
                        put_split(high, low, q, phase, piece)
    inter = interleave_hot(5, True)
    for q in range(8):
        rows = slice(q * 128, (q + 1) * 128)
        grad_ref[:, q * 512 : (q + 1) * 512] = dot(high[rows, :], inter) + dot(low[rows, :], inter)


def put_split(high, low, q, phase, piece):
    rounded = piece.astype(bf16)
    high[q * 128 : (q + 1) * 128, phase * 128 : (phase + 1) * 128] = rounded
    low[q * 128 : (q + 1) * 128, phase * 128 : (phase + 1) * 128] = (
        piece - rounded.astype(f32)
    ).astype(bf16)


def second_halo_body(
    one_ref, two_ref, kern_ref, act_up_ref, taps_in_ref,
    grad_ref, taps_ref, below_ref, high, low, phase_buf, cols_buf,
):
    one, two = (one_ref[...].astype(f32), two_ref[...].astype(f32))
    odd = (lax.axis_index("slab") & 1).astype(f32)
    above = (one + odd * (two - one)).astype(bf16)
    below_rows((two + odd * (one - two))[0:128], below_ref, phase_buf, cols_buf)
    taps = jnp.zeros((256, 256), f32)
    grid = []
    for v, (row_off, col_off) in enumerate(variants):
        wide = dot(above, spread_hot(row_off, col_off))
        match = wide[:, 256:512] == cell_of(row_off, col_off)
        grid.append(jnp.where(match, wide[:, 0:256], 0.0).astype(bf16))
        part = taps_in_ref[v] + dot_lanes(grid[v], act_up_ref[:, 256:512])
        taps = taps + dot(part.astype(bf16), second_hot(row_off, col_off))
    taps_ref[...] = taps.astype(bf16)
    for row_phase in range(2):
        for col_phase in range(2):
            total = jnp.zeros((128, 256), f32)
            for row_tap, row_off in phase_taps[row_phase]:
                for col_tap, col_off in phase_taps[col_phase]:
                    total = total + dot(kern_ref[3 * row_tap + col_tap], grid[row_off * 2 + col_off])
            for half in range(2):
                put_split(high, low, half, row_phase * 2 + col_phase, total[:, half * 128 : half * 128 + 128])
    inter = interleave_hot(5, True)
    for q in range(2):
        rows = slice(q * 128, (q + 1) * 128)
        grad_ref[:, q * 512 : (q + 1) * 512] = dot(high[rows, :], inter) + dot(low[rows, :], inter)


def next_col(value):
    lane = lanes_of(value.shape[1])
    return jnp.where((lane & 31) < 31, pltpu.roll(value, value.shape[1] - 1, 1), 0.0)


def next_row(value):
    lane = lanes_of(value.shape[1])
    return jnp.where(((lane >> 5) & 31) < 31, pltpu.roll(value, value.shape[1] - 32, 1), 0.0)


def fold_taps(wide):
    def group(row_tap, col_tap):
        at = (row_tap * 3 + col_tap) * 8
        return wide[at : at + 8, :]

    return (
        group(1, 1),
        group(1, 2) + next_col(group(1, 0)),
        group(2, 1) + next_row(group(0, 1)),
        group(2, 2) + next_col(group(2, 0)) + next_row(group(0, 2) + next_col(group(0, 0))),
    )


def first_taps_body(
    p0_ref, p1_ref, p2_ref, p3_ref, grad_ref, halo_ref, cols_ref, below_ref, second_ref, kern_ref,
    first_ref, kept_ref, sent_ref, edge_ref, buf, taps_buf,
):
    for col_step, ref in enumerate((p0_ref, p1_ref, p2_ref, p3_ref)):
        slope = slope_of(ref[...].astype(f32))
        for row_step in range(4):
            at = pl.multiple_of(channel_block(col_step, row_step) * 8, 8)
            rows = slope[row_step * 8 : (row_step + 1) * 8, :]
            buf[pl.ds(at, 8), 0:3072] = grad_ref[pl.ds(at, 8), 0:3072] * rows[:, 0:3072]
            last = grad_ref[pl.ds(at, 8), 3072:4096] + halo_ref[pl.ds(at, 8), :]
            buf[pl.ds(at, 8), 3072:4096] = last * rows[:, 3072:4096]
    grad = buf[...].astype(bf16)
    first_ref[0:128, :] = grad
    first_ref[128:256, 0:3072] = grad[:, 1024:4096]
    first_ref[128:256, 3072:4096] = jnp.zeros((128, 1024), bf16)
    taps = dot_lanes(first_ref[0:128, :], cols_ref[...])
    taps = (taps + dot_lanes(first_ref[0:128, 0:1024], below_ref[...])).astype(bf16)
    taps_buf[...] = dot(taps, first_hot())
    core = lax.axis_index("slab") & 1
    for pair in range(8):
        for ref, which in ((kept_ref, core), (sent_ref, 1 - core)):
            slab = pair * 2 + which
            ref[pair, :, 0:256] = second_ref[pl.ds(pl.multiple_of(slab * 16, 16), 16), :]
            part = taps_buf[pl.ds(pl.multiple_of(slab * 8, 8), 8), :]
            ref[pair, :, 256:384] = jnp.concatenate([part, jnp.zeros((8, 128), f32)], 0).astype(bf16)
    edges = fold_taps(dot(kern_ref[:, 128:256], first_ref[0:128, 0:1024]))
    edge_ref[...] = jnp.concatenate([edge[4:8, :] for edge in edges], 0).astype(bf16)


def first_body(first_ref, kern_ref, edge_ref, out_ref, buf):
    phases = fold_taps(dot(kern_ref[...], first_ref[...]))
    edge = edge_ref[...].astype(f32)
    for t in range(32):
        for phase in range(4):
            value = phases[phase][:, t * 128 : (t + 1) * 128]
            if t >= 24:
                lane = (t - 24) * 128
                extra = edge[phase * 4 : (phase + 1) * 4, lane : lane + 128]
                value = value + jnp.concatenate([jnp.zeros((4, 128), f32), extra], 0)
            buf[t * 8 : (t + 1) * 8, phase * 128 : (phase + 1) * 128] = value
    ordered = dot(row_hot(False), buf[...].astype(bf16)).astype(bf16)
    natural = dot(ordered, interleave_hot(6, True))
    for g in range(8):
        for channel in range(4):
            at = g * 32 + channel * 8
            out_ref[0, channel, :, g * 512 : (g + 1) * 512] = natural[at : at + 8, :].astype(bf16)


def middle_body(kept_ref, came_ref, next_ref, s1_ref, s2_ref, s3_ref):
    y = (lax.axis_index("slab") >> 1) & 3
    for z in range(2):
        for step, ref in enumerate((next_ref, s1_ref, s2_ref, s3_ref)):
            at = z * 4 + ((y + step) & 3)
            value = kept_ref[at].astype(f32) + came_ref[at].astype(f32)
            ref[z] = value.astype(ref.dtype)


def late_body(kept_ref, c1_ref, c2_ref, c3_ref, next_ref, sent_ref):
    z = lax.axis_index("slab") >> 3

    def total(at):
        value = kept_ref[at]
        for ref in (c1_ref, c2_ref, c3_ref):
            value = value + ref[at].astype(f32)
        return value

    next_ref[...] = total(z)
    sent_ref[...] = total(1 - z).astype(bf16)


def final_body(kept_ref, came_ref, first_ref, second_ref):
    total = kept_ref[...] + came_ref[...].astype(f32)
    for channel in range(8):
        at = channel * 32
        second_ref[channel] = total[:, at : at + 27] * (1.0 / math.sqrt(1024.0))
    for channel in range(4):
        at = 256 + channel * 32
        first_ref[channel] = total[0:8, at : at + 27] * (1.0 / math.sqrt(65536.0))


def call(body, out, scratch=(), micros=0.05, limit=16, **options):
    return pl.pallas_call(
        body,
        out_shape=out,
        scratch_shapes=list(scratch),
        compiler_params=pltpu.CompilerParams(vmem_limit_bytes=limit * 1024 * 1024),
        cost_estimate=pl.CostEstimate(
            flops=int(micros * 1.0e9), bytes_accessed=100000, transcendentals=0
        ),
        **options,
    )


def shape(dims, dtype=bf16):
    return jax.ShapeDtypeStruct(dims, dtype)


def from_ahead_x(value, step):
    return lax.ppermute(
        value, "chan", [((s // 4) * 4 + (s % 4 + step) % 4, s) for s in range(16)]
    )


def from_ahead_z(value, step):
    return lax.ppermute(value, "chan", [((s + 4 * step) % 16, s) for s in range(16)])


def gather(value, exchange):
    return [value] + [exchange(value, step) for step in (1, 2, 3)]


def from_above(value):
    return lax.ppermute(value, "slab", [(s, s - 1) for s in range(1, 16)])


def swap_next(value):
    pairs = [(s, s + 1) for s in range(1, 14, 2)] + [(s + 1, s) for s in range(1, 14, 2)]
    return lax.ppermute(value, "slab", pairs)


def swap(value, axis, mask):
    return lax.ppermute(value, axis, [(s, s ^ mask) for s in range(16)])


def on_device(
    volume_in, pre_first, pre_second, kernel_first, kernel_second, pool_index, grad_pooled
):
    message = call(
        pool_body,
        shape((8, 4352)),
        (
            pltpu.VMEM((1, 16, 2, 256), bf16),
            pltpu.VMEM((1, 16, 1, 64), jnp.int32),
            pltpu.VMEM((16, 64), bf16),
            pltpu.VMEM((1, 8, 4, 1024), bf16),
            pltpu.SemaphoreType.DMA((4,)),
        ),
        limit=60,
        in_specs=[pl.BlockSpec(memory_space=pltpu.HBM)] * 4,
    )(pre_second, pool_index, grad_pooled.reshape(16, 64), pre_first)
    kernel_second = call(hold_body, shape((27, 128, 256)))(kernel_second)
    own_kernel = lax.dynamic_slice_in_dim(kernel_first, lax.axis_index("chan") * 4, 4, 1)
    act, act_up, cols, kern, top = call(
        local_body,
        (shape((128, 512)), shape((128, 512)), shape((128, 4096)), shape((72, 256)), shape((128, 128))),
        (
            pltpu.VMEM((256, 512), f32),
            pltpu.VMEM((32, 4096), f32),
            pltpu.VMEM((128, 4096), f32),
            pltpu.VMEM((72, 256), f32),
            pltpu.VMEM((128, 128), f32),
        ),
    )(message, volume_in.reshape(32, 4096), own_kernel)

    whole = pl.BlockSpec(memory_space=pltpu.VMEM)
    unread = pl.BlockSpec(memory_space=pl.ANY)
    messages = gather(message, from_ahead_z)
    small = call(join_small_body, shape((64, 128)), in_specs=[whole] * 4 + [unread] * 2)(
        *messages, top, kernel_second
    )
    block = (256, 128)
    small, one, two = call(order_body, (shape(block), shape(block), shape(block)))(
        *gather(small, from_ahead_x), top
    )
    pre_all = gather(call(join_body, shape((32, 4096)))(*messages), from_ahead_x)
    one, two = (swap(one, "slab", 1), swap_next(two))
    grad_act, second = call(
        second_body,
        (shape((128, 4096), f32), shape((4, 256, 128), f32)),
        (pltpu.VMEM((4, 256, 512), bf16), pltpu.VMEM((1024, 512), bf16), pltpu.VMEM((1024, 512), bf16)),
        micros=3.0,
    )(small, kernel_second, act, act_up)
    grad_halo, second, below = call(
        second_halo_body,
        (shape((128, 1024), f32), shape((256, 256)), shape((128, 1024))),
        (
            pltpu.VMEM((256, 512), bf16),
            pltpu.VMEM((256, 512), bf16),
            pltpu.VMEM((32, 1024), f32),
            pltpu.VMEM((128, 1024), f32),
        ),
        micros=2.0,
    )(one, two, kernel_second, act_up, second)
    grad_first, kept, sent, edge = call(
        first_taps_body,
        (shape((256, 4096)), shape((8, 16, 384)), shape((8, 16, 384)), shape((16, 1024))),
        (pltpu.VMEM((128, 4096), f32), pltpu.VMEM((128, 128), f32)),
    )(*pre_all, grad_act, grad_halo, cols, below, second, kern)

    block = (2, 16, 384)
    kept, *sent = call(
        middle_body, (shape(block, f32), shape(block), shape(block), shape(block))
    )(kept, swap(sent, "slab", 1))
    came = []
    for step in (1, 2, 3):
        pairs = [(s, (s & 9) | ((((s >> 1) + step) & 3) << 1)) for s in range(16)]
        came.append(lax.ppermute(sent[step - 1], "slab", pairs))
    kept, sent = call(late_body, (shape((16, 384), f32), shape((16, 384))))(kept, *came)
    grad_volume = call(first_body, shape((1, 4, 8, 4096)), (pltpu.VMEM((256, 512), f32),))(
        grad_first, kern, from_above(edge)
    )
    weight_first, weight_second = call(
        final_body, (shape((4, 8, 27), f32), shape((8, 16, 27), f32))
    )(kept, swap(sent, "slab", 8))
    return (
        grad_volume,
        jnp.transpose(weight_first, (2, 0, 1)),
        jnp.transpose(weight_second, (2, 0, 1)),
    )


def solution(mesh):
    return jax.shard_map(
        on_device,
        mesh=mesh,
        in_specs=(
            P(None, "chan", "slab", None),
            P(None, "chan", "slab", None),
            P(None, "chan", "slab", None),
            P(),
            P(),
            P(None, "chan", "slab", None),
            P(None, "chan", "slab", None),
        ),
        out_specs=(P(None, "chan", "slab", None), P(None, "chan", "slab"), P(None, "chan", "slab")),
        check_vma=False,
    )
```

```python
import math

import jax
import jax.numpy as jnp
from jax import lax
from jax.experimental import pallas as pl
from jax.experimental.pallas import tpu as pltpu
from jax.sharding import PartitionSpec as P

H = 64
leaky_slope = 0.2
bf16 = jnp.bfloat16
f32 = jnp.float32
variants = ((0, 0), (0, 1), (1, 0), (1, 1))
phase_taps = (((1, 0),), ((2, 0), (0, 1)))


def index_of(shape, dim):
    return lax.broadcasted_iota(jnp.int32, shape, dim)


def rows_of(count):
    return index_of((count, 1), 0)


def lanes_of(count):
    return index_of((1, count), 1)


def one_hot(match):
    return jnp.where(match, 1.0, 0.0).astype(bf16)


def interleave_hot(log_width, to_natural):
    natural = lanes_of(512) if to_natural else rows_of(512)
    row, col = (natural >> log_width, natural & ((1 << log_width) - 1))
    source = ((row & 1) << 8) | ((col & 1) << 7) | ((row >> 1) << (log_width - 1)) | (col >> 1)
    return one_hot(source == index_of((512, 512), 0 if to_natural else 1))


def spread_hot(row_off, col_off):
    lane = lanes_of(512)
    row, col = (((lane >> 4) & 15) + row_off, (lane & 15) + col_off)
    window = ((row >> 1) << 3) + (col >> 1) + ((lane >> 8) << 6)
    window = jnp.where((row < 16) & (col < 16), window, -1)
    return one_hot(window == index_of((128, 512), 0))


def row_hot(to_grouped):
    new = rows_of(256) if to_grouped else lanes_of(256)
    source = (((new >> 3) & 7) << 5) | ((new & 3) << 3) | ((new >> 6) << 1) | ((new >> 2) & 1)
    return one_hot(source == index_of((256, 256), 1 if to_grouped else 0))


def halo_hot():
    new, old = (index_of((64, 32), 0), index_of((64, 32), 1))
    return one_hot((((new >> 3) << 2 | (new & 3)) == old) & ((new & 4) == 4))


def second_hot(row_off, col_off):
    row = rows_of(128)
    group, row_phase, col_phase = (row >> 5, (row >> 4) & 1, (row >> 3) & 1)
    depth_tap = jnp.where(group == 2, 0, group + 1)
    row_tap = 0 if row_off else 1 + row_phase
    col_tap = 0 if col_off else 1 + col_phase
    target = ((row & 7) << 5) + 9 * depth_tap + 3 * row_tap + col_tap
    valid = (group < 3) & (row_phase >= row_off) & (col_phase >= col_off)
    return one_hot(jnp.where(valid, target, -1) == index_of((128, 256), 1))


def first_hot():
    row = rows_of(128)
    tap = jnp.where(row < 72, 9 + 9 * ((row >> 2) & 1) + (row >> 3), (row - 72) >> 2)
    target = jnp.where(row < 108, ((row & 3) << 5) + tap, -1)
    return one_hot(target == index_of((128, 128), 1))


def dot(left, right):
    return jnp.dot(left, right, preferred_element_type=f32)


def dot_lanes(left, right):
    return lax.dot_general(left, right, (((1,), (1,)), ((), ())), preferred_element_type=f32)


def slope_of(values):
    return jnp.where(values > 0, 1.0, leaky_slope).astype(f32)


def cell_of(row_off, col_off):
    lane = lanes_of(256)
    cell = (((lane >> 4) + row_off) & 1) * 2 + ((lane + col_off) & 1)
    return cell.astype(f32)


def plane_of(value, plane):
    return jnp.sum(jnp.where(index_of(value.shape, 1) == plane, value, 0.0), axis=1)


def pool_body(
    pre_hbm, index_hbm, grad_hbm, first_hbm, out_ref, pre_ref, index_ref, grad_ref, first_ref, sems
):
    copies = [
        pltpu.make_async_copy(source, target, sems.at[i])
        for i, (source, target) in enumerate(
            ((first_hbm, first_ref), (pre_hbm, pre_ref), (index_hbm, index_ref), (grad_hbm, grad_ref))
        )
    ]
    for copy in copies:
        copy.start()
    cell = cell_of(0, 0)
    lane = lanes_of(256)
    spread = one_hot((((lane >> 5) << 3) | ((lane >> 1) & 7)) == index_of((64, 256), 0))
    lane = rows_of(256)
    back = one_hot((((lane >> 5) << 3) | ((lane >> 1) & 7)) == index_of((256, 128), 1))
    tag = one_hot(rows_of(64) + 64 == index_of((64, 128), 1))
    for copy in copies:
        copy.wait()
    for plane in range(4):
        out_ref[:, plane * 1024 : (plane + 1) * 1024] = first_ref[0, :, plane, :]
    index = index_ref[0, :, 0, :].astype(f32).astype(bf16)
    both = jnp.concatenate([grad_ref[...], index], 0)
    both = dot(both, spread)
    total = jnp.zeros((16, 256), f32)
    for depth in range(2):
        pre = pre_ref[0, :, depth, :].astype(f32)
        total = total + jnp.where(both[16:32] == cell + 4.0 * depth, both[0:16] * slope_of(pre), 0.0)
    small = dot(total.astype(bf16), back) + dot(index, tag)
    out_ref[:, 4096:4224] = small[0:8].astype(bf16)
    out_ref[:, 4224:4352] = small[8:16].astype(bf16)


def hold_body(kern_ref, out_ref):
    out_ref[...] = kern_ref[...]


def tap_rows(phases):
    lane = lanes_of(phases.shape[1])
    has_col = (lane & 31) > 0
    has_row = ((lane >> 5) & 31) > 0
    result = []
    for row_tap in range(3):
        row_phase = 0 if row_tap == 1 else 1
        for col_tap in range(3):
            col_phase = 0 if col_tap == 1 else 1
            phase = row_phase * 2 + col_phase
            value = phases[phase * 8 : phase * 8 + 8, :]
            if col_tap == 0:
                value = jnp.where(has_col, pltpu.roll(value, 1, 1), 0.0)
            if row_tap == 0:
                value = jnp.where(has_row, pltpu.roll(value, 32, 1), 0.0)
            result.append(value)
    return result


def below_rows(halo, out_ref, phase_buf, cols_buf):
    halo = jnp.concatenate([halo[part * 32 : (part + 1) * 32] for part in range(4)], 1)
    halo = dot(halo_hot(), dot(halo.astype(bf16), interleave_hot(6, False)).astype(bf16))
    for t in range(8):
        for phase in range(4):
            phase_buf[phase * 8 : phase * 8 + 8, t * 128 : (t + 1) * 128] = halo[
                t * 8 : t * 8 + 8, phase * 128 : (phase + 1) * 128
            ]
    cols_buf[...] = jnp.zeros_like(cols_buf)
    for tap, value in enumerate(tap_rows(phase_buf)):
        cols_buf[72 + tap * 4 : 76 + tap * 4, :] = value[4:8, :]
    out_ref[...] = cols_buf[...].astype(bf16)


def local_body(
    pre_ref, vol_ref, kern_ref,
    act_ref, act_up_ref, cols_ref, kern_out_ref, top_ref, act_buf, phase_buf, cols_buf, kern_buf, top_buf,
):
    pre = pre_ref[:, 0:4096].astype(f32)
    act = jnp.where(pre > 0, pre, leaky_slope * pre)
    stacked = jnp.concatenate([act[:, q * 512 : (q + 1) * 512] for q in range(8)], 0)
    split = dot(stacked.astype(bf16), interleave_hot(5, False))
    act_buf[...] = jnp.zeros_like(act_buf)
    for q in range(8):
        plane, half = (q // 2, q % 2)
        pair, parity = (plane // 2, plane % 2)
        for phase in range(4):
            row = (parity * 4 + phase) * 8
            lane = pair * 256 + half * 128
            piece = split[q * 8 : (q + 1) * 8, phase * 128 : (phase + 1) * 128]
            act_buf[row : row + 8, lane : lane + 128] = piece
            if parity == 1:
                row = 128 + 64 + phase * 8
                act_buf[row : row + 8, lane : lane + 128] = piece
    act_ref[...] = act_buf[0:128, :].astype(bf16)
    act_up_ref[...] = act_buf[128:256, :].astype(bf16)

    split_zero = interleave_hot(6, False)
    wide = jnp.concatenate([vol_ref[:, g * 512 : (g + 1) * 512] for g in range(8)], 0)
    ordered = dot(row_hot(True), dot(wide, split_zero).astype(bf16))
    for t in range(32):
        for phase in range(4):
            phase_buf[phase * 8 : phase * 8 + 8, t * 128 : (t + 1) * 128] = ordered[
                t * 8 : t * 8 + 8, phase * 128 : (phase + 1) * 128
            ]
    cols_buf[72:128, :] = jnp.zeros((56, 4096), f32)
    for tap, value in enumerate(tap_rows(phase_buf)):
        cols_buf[tap * 8 : tap * 8 + 8, :] = value
        cols_buf[72 + tap * 4 : 76 + tap * 4, 1024:4096] = value[4:8, 0:3072]
    cols_ref[...] = cols_buf[...].astype(bf16)
    top = plane_of(vol_ref[...].astype(f32).reshape(4, 8, 4096), 7)
    for part in range(4):
        for g in range(8):
            lane = (g * 4 + part) * 128
            top_buf[part * 32 + g * 4 : part * 32 + g * 4 + 4, :] = top[:, lane : lane + 128]
    top_ref[...] = top_buf[...].astype(bf16)

    kern_buf[...] = jnp.zeros_like(kern_buf)
    for tap in range(9):
        kern_buf[tap * 8 : tap * 8 + 4, 0:128] = kern_ref[9 + tap].astype(f32)
        kern_buf[tap * 8 + 4 : tap * 8 + 8, 0:128] = kern_ref[18 + tap].astype(f32)
        kern_buf[tap * 8 + 4 : tap * 8 + 8, 128:256] = kern_ref[tap].astype(f32)
    kern_out_ref[...] = kern_buf[...].astype(bf16)


def channel_block(col_step, row_step):
    me = lax.axis_index("chan")
    return (((me >> 2) + row_step) & 3) * 4 + (((me & 3) + col_step) & 3)


def join_small_body(m0_ref, m1_ref, m2_ref, m3_ref, after_ref, table_ref, out_ref):
    for step, ref in enumerate((m0_ref, m1_ref, m2_ref, m3_ref)):
        rows = jnp.concatenate([ref[:, 4096:4224].astype(f32), ref[:, 4224:4352].astype(f32)], 0)
        out_ref[step * 16 : step * 16 + 16, :] = rows.astype(bf16)


def join_body(m0_ref, m1_ref, m2_ref, m3_ref, out_ref):
    rows = [ref[:, 0:4096].astype(f32) for ref in (m0_ref, m1_ref, m2_ref, m3_ref)]
    out_ref[...] = jnp.concatenate(rows, 0).astype(bf16)


def order_body(s0_ref, s1_ref, s2_ref, s3_ref, top_ref, out_ref, one_ref, two_ref):
    for col_step, ref in enumerate((s0_ref, s1_ref, s2_ref, s3_ref)):
        for row_step in range(4):
            at = pl.multiple_of(channel_block(col_step, row_step) * 16, 16)
            out_ref[pl.ds(at, 16), :] = ref[row_step * 16 : row_step * 16 + 16, :]
    up = jnp.concatenate([top_ref[...].astype(f32), jnp.zeros((128, 128), f32)], 0)
    down = out_ref[...].astype(f32)
    odd = (lax.axis_index("slab") & 1).astype(f32)
    one_ref[...] = (up + odd * (down - up)).astype(bf16)
    two_ref[...] = (down + odd * (up - down)).astype(bf16)


def second_body(
    small_ref, kern_ref, act_ref, act_up_ref, grad_ref, taps_ref, grid, high, low
):
    small = small_ref[...]
    for v, (row_off, col_off) in enumerate(variants):
        wide = dot(small, spread_hot(row_off, col_off))
        cell = cell_of(row_off, col_off)
        for plane in range(2):
            match = wide[:, 256:512] == cell + 4.0 * plane
            grid[v, :, plane * 256 : (plane + 1) * 256] = jnp.where(
                match, wide[:, 0:256], 0.0
            ).astype(bf16)
    for v in range(4):
        taps_ref[v] = dot_lanes(grid[v], act_ref[...]) + dot_lanes(
            grid[v, :, 256:512], act_up_ref[:, 0:256]
        )
    for depth_phase in range(2):
        for row_phase in range(2):
            for col_phase in range(2):
                total = jnp.zeros((128, 512), f32)
                ahead = jnp.zeros((128, 256), f32)
                for row_tap, row_off in phase_taps[row_phase]:
                    for col_tap, col_off in phase_taps[col_phase]:
                        tap = 3 * row_tap + col_tap
                        v = row_off * 2 + col_off
                        total = total + dot(kern_ref[9 + 9 * depth_phase + tap], grid[v])
                        if depth_phase == 1:
                            ahead = ahead + dot(kern_ref[tap], grid[v, :, 256:512])
                phase = row_phase * 2 + col_phase
                for pair in range(2):
                    for half in range(2):
                        q = (2 * pair + depth_phase) * 2 + half
                        lane = pair * 256 + half * 128
                        piece = total[:, lane : lane + 128]
                        if pair == 0 and depth_phase == 1:
                            piece = piece + ahead[:, lane : lane + 128]
                        put_split(high, low, q, phase, piece)
    inter = interleave_hot(5, True)
    for q in range(8):
        rows = slice(q * 128, (q + 1) * 128)
        grad_ref[:, q * 512 : (q + 1) * 512] = dot(high[rows, :], inter) + dot(low[rows, :], inter)


def put_split(high, low, q, phase, piece):
    rounded = piece.astype(bf16)
    high[q * 128 : (q + 1) * 128, phase * 128 : (phase + 1) * 128] = rounded
    low[q * 128 : (q + 1) * 128, phase * 128 : (phase + 1) * 128] = (
        piece - rounded.astype(f32)
    ).astype(bf16)


def second_halo_body(
    one_ref, two_ref, kern_ref, act_up_ref, taps_in_ref,
    grad_ref, taps_ref, below_ref, high, low, phase_buf, cols_buf,
):
    one, two = (one_ref[...].astype(f32), two_ref[...].astype(f32))
    odd = (lax.axis_index("slab") & 1).astype(f32)
    above = (one + odd * (two - one)).astype(bf16)
    below_rows((two + odd * (one - two))[0:128], below_ref, phase_buf, cols_buf)
    taps = jnp.zeros((256, 256), f32)
    grid = []
    for v, (row_off, col_off) in enumerate(variants):
        wide = dot(above, spread_hot(row_off, col_off))
        match = wide[:, 256:512] == cell_of(row_off, col_off)
        grid.append(jnp.where(match, wide[:, 0:256], 0.0).astype(bf16))
        part = taps_in_ref[v] + dot_lanes(grid[v], act_up_ref[:, 256:512])
        taps = taps + dot(part.astype(bf16), second_hot(row_off, col_off))
    taps_ref[...] = taps.astype(bf16)
    for row_phase in range(2):
        for col_phase in range(2):
            total = jnp.zeros((128, 256), f32)
            for row_tap, row_off in phase_taps[row_phase]:
                for col_tap, col_off in phase_taps[col_phase]:
                    total = total + dot(kern_ref[3 * row_tap + col_tap], grid[row_off * 2 + col_off])
            for half in range(2):
                put_split(high, low, half, row_phase * 2 + col_phase, total[:, half * 128 : half * 128 + 128])
    inter = interleave_hot(5, True)
    for q in range(2):
        rows = slice(q * 128, (q + 1) * 128)
        grad_ref[:, q * 512 : (q + 1) * 512] = dot(high[rows, :], inter) + dot(low[rows, :], inter)


def next_col(value):
    lane = lanes_of(value.shape[1])
    return jnp.where((lane & 31) < 31, pltpu.roll(value, value.shape[1] - 1, 1), 0.0)


def next_row(value):
    lane = lanes_of(value.shape[1])
    return jnp.where(((lane >> 5) & 31) < 31, pltpu.roll(value, value.shape[1] - 32, 1), 0.0)


def fold_taps(wide):
    def group(row_tap, col_tap):
        at = (row_tap * 3 + col_tap) * 8
        return wide[at : at + 8, :]

    return (
        group(1, 1),
        group(1, 2) + next_col(group(1, 0)),
        group(2, 1) + next_row(group(0, 1)),
        group(2, 2) + next_col(group(2, 0)) + next_row(group(0, 2) + next_col(group(0, 0))),
    )


def first_taps_body(
    p0_ref, p1_ref, p2_ref, p3_ref, grad_ref, halo_ref, cols_ref, below_ref, second_ref,
    first_ref, kept_ref, sent_ref, buf, taps_buf,
):
    for col_step, ref in enumerate((p0_ref, p1_ref, p2_ref, p3_ref)):
        slope = slope_of(ref[...].astype(f32))
        for row_step in range(4):
            at = pl.multiple_of(channel_block(col_step, row_step) * 8, 8)
            rows = slope[row_step * 8 : (row_step + 1) * 8, :]
            buf[pl.ds(at, 8), 0:3072] = grad_ref[pl.ds(at, 8), 0:3072] * rows[:, 0:3072]
            last = grad_ref[pl.ds(at, 8), 3072:4096] + halo_ref[pl.ds(at, 8), :]
            buf[pl.ds(at, 8), 3072:4096] = last * rows[:, 3072:4096]
    first_ref[...] = buf[...].astype(bf16)
    taps = dot_lanes(first_ref[...], cols_ref[...])
    taps = (taps + dot_lanes(first_ref[:, 0:1024], below_ref[...])).astype(bf16)
    taps_buf[...] = dot(taps, first_hot())
    core = lax.axis_index("slab") & 1
    for pair in range(8):
        for ref, which in ((kept_ref, core), (sent_ref, 1 - core)):
            slab = pair * 2 + which
            ref[pair, :, 0:256] = second_ref[pl.ds(pl.multiple_of(slab * 16, 16), 16), :]
            part = taps_buf[pl.ds(pl.multiple_of(slab * 8, 8), 8), :]
            ref[pair, :, 256:384] = jnp.concatenate([part, jnp.zeros((8, 128), f32)], 0).astype(bf16)


def edge_body(first_ref, kern_ref, out_ref):
    edges = fold_taps(dot(kern_ref[:, 128:256], first_ref[:, 0:1024]))
    out_ref[...] = jnp.concatenate([edge[4:8, :] for edge in edges], 0).astype(bf16)


def first_body(first_ref, kern_ref, edge_ref, out_ref, buf):
    ahead = dot(kern_ref[:, 128:256], first_ref[:, 1024:4096])
    ahead = jnp.concatenate([ahead, jnp.zeros((72, 1024), f32)], 1)
    phases = fold_taps(dot(kern_ref[:, 0:128], first_ref[...]) + ahead)
    edge = edge_ref[...].astype(f32)
    for t in range(32):
        for phase in range(4):
            value = phases[phase][:, t * 128 : (t + 1) * 128]
            if t >= 24:
                lane = (t - 24) * 128
                extra = edge[phase * 4 : (phase + 1) * 4, lane : lane + 128]
                value = value + jnp.concatenate([jnp.zeros((4, 128), f32), extra], 0)
            buf[t * 8 : (t + 1) * 8, phase * 128 : (phase + 1) * 128] = value
    ordered = dot(row_hot(False), buf[...].astype(bf16)).astype(bf16)
    natural = dot(ordered, interleave_hot(6, True))
    for g in range(8):
        for channel in range(4):
            at = g * 32 + channel * 8
            out_ref[0, channel, :, g * 512 : (g + 1) * 512] = natural[at : at + 8, :].astype(bf16)


def middle_body(kept_ref, came_ref, edge_ref, next_ref, s1_ref, s2_ref, s3_ref):
    y = (lax.axis_index("slab") >> 1) & 3
    for z in range(2):
        for step, ref in enumerate((next_ref, s1_ref, s2_ref, s3_ref)):
            at = z * 4 + ((y + step) & 3)
            value = kept_ref[at].astype(f32) + came_ref[at].astype(f32)
            ref[z] = value.astype(ref.dtype)


def late_body(kept_ref, c1_ref, c2_ref, c3_ref, next_ref, sent_ref):
    z = lax.axis_index("slab") >> 3

    def total(at):
        value = kept_ref[at]
        for ref in (c1_ref, c2_ref, c3_ref):
            value = value + ref[at].astype(f32)
        return value

    next_ref[...] = total(z)
    sent_ref[...] = total(1 - z).astype(bf16)


def final_body(kept_ref, came_ref, first_ref, second_ref):
    total = kept_ref[...] + came_ref[...].astype(f32)
    for channel in range(8):
        at = channel * 32
        second_ref[channel] = total[:, at : at + 27] * (1.0 / math.sqrt(1024.0))
    for channel in range(4):
        at = 256 + channel * 32
        first_ref[channel] = total[0:8, at : at + 27] * (1.0 / math.sqrt(65536.0))


def call(body, out, scratch=(), micros=0.05, limit=16, **options):
    return pl.pallas_call(
        body,
        out_shape=out,
        scratch_shapes=list(scratch),
        compiler_params=pltpu.CompilerParams(vmem_limit_bytes=limit * 1024 * 1024),
        cost_estimate=pl.CostEstimate(
            flops=int(micros * 1.0e9), bytes_accessed=100000, transcendentals=0
        ),
        **options,
    )


def shape(dims, dtype=bf16):
    return jax.ShapeDtypeStruct(dims, dtype)


def from_ahead_x(value, step):
    return lax.ppermute(
        value, "chan", [((s // 4) * 4 + (s % 4 + step) % 4, s) for s in range(16)]
    )


def from_ahead_z(value, step):
    return lax.ppermute(value, "chan", [((s + 4 * step) % 16, s) for s in range(16)])


def gather(value, exchange):
    came = {step: exchange(value, step) for step in (1, 2, 3)}
    return [value, came[1], came[2], came[3]]


def from_above(value):
    return lax.ppermute(value, "slab", [(s, s - 1) for s in range(1, 16)])


def swap_next(value):
    pairs = [(s, s + 1) for s in range(1, 14, 2)] + [(s + 1, s) for s in range(1, 14, 2)]
    return lax.ppermute(value, "slab", pairs)


def swap(value, axis, mask):
    return lax.ppermute(value, axis, [(s, s ^ mask) for s in range(16)])


def on_device(
    volume_in, pre_first, pre_second, kernel_first, kernel_second, pool_index, grad_pooled
):
    message = call(
        pool_body,
        shape((8, 4352)),
        (
            pltpu.VMEM((1, 16, 2, 256), bf16),
            pltpu.VMEM((1, 16, 1, 64), jnp.int32),
            pltpu.VMEM((16, 64), bf16),
            pltpu.VMEM((1, 8, 4, 1024), bf16),
            pltpu.SemaphoreType.DMA((4,)),
        ),
        limit=60,
        in_specs=[pl.BlockSpec(memory_space=pltpu.HBM)] * 4,
    )(pre_second, pool_index, grad_pooled.reshape(16, 64), pre_first)
    kernel_second = call(hold_body, shape((27, 128, 256)))(kernel_second)
    own_kernel = lax.dynamic_slice_in_dim(kernel_first, lax.axis_index("chan") * 4, 4, 1)
    act, act_up, cols, kern, top = call(
        local_body,
        (shape((128, 512)), shape((128, 512)), shape((128, 4096)), shape((72, 256)), shape((128, 128))),
        (
            pltpu.VMEM((256, 512), f32),
            pltpu.VMEM((32, 4096), f32),
            pltpu.VMEM((128, 4096), f32),
            pltpu.VMEM((72, 256), f32),
            pltpu.VMEM((128, 128), f32),
        ),
    )(message, volume_in.reshape(32, 4096), own_kernel)

    whole = pl.BlockSpec(memory_space=pltpu.VMEM)
    unread = pl.BlockSpec(memory_space=pl.ANY)
    messages = gather(message, from_ahead_z)
    small = call(join_small_body, shape((64, 128)), in_specs=[whole] * 4 + [unread] * 2)(
        *messages, top, kernel_second
    )
    block = (256, 128)
    small, one, two = call(order_body, (shape(block), shape(block), shape(block)))(
        *gather(small, from_ahead_x), top
    )
    pre_all = gather(call(join_body, shape((32, 4096)))(*messages), from_ahead_x)
    one, two = (swap(one, "slab", 1), swap_next(two))
    grad_act, second = call(
        second_body,
        (shape((128, 4096), f32), shape((4, 256, 128), f32)),
        (pltpu.VMEM((4, 256, 512), bf16), pltpu.VMEM((1024, 512), bf16), pltpu.VMEM((1024, 512), bf16)),
        micros=3.0,
    )(small, kernel_second, act, act_up)
    grad_halo, second, below = call(
        second_halo_body,
        (shape((128, 1024), f32), shape((256, 256)), shape((128, 1024))),
        (
            pltpu.VMEM((256, 512), bf16),
            pltpu.VMEM((256, 512), bf16),
            pltpu.VMEM((32, 1024), f32),
            pltpu.VMEM((128, 1024), f32),
        ),
        micros=2.0,
    )(one, two, kernel_second, act_up, second)
    grad_first, kept, sent = call(
        first_taps_body,
        (shape((128, 4096)), shape((8, 16, 384)), shape((8, 16, 384))),
        (pltpu.VMEM((128, 4096), f32), pltpu.VMEM((128, 128), f32)),
    )(*pre_all, grad_act, grad_halo, cols, below, second)
    edge = call(edge_body, shape((16, 1024)))(grad_first, kern)

    block = (2, 16, 384)
    kept, *sent = call(
        middle_body,
        (shape(block, f32), shape(block), shape(block), shape(block)),
        in_specs=[whole, whole, unread],
    )(kept, swap(sent, "slab", 1), edge)
    came = []
    for step in (1, 2, 3):
        pairs = [(s, (s & 9) | ((((s >> 1) + step) & 3) << 1)) for s in range(16)]
        came.append(lax.ppermute(sent[step - 1], "slab", pairs))
    kept, sent = call(late_body, (shape((16, 384), f32), shape((16, 384))))(kept, *came)
    grad_volume = call(first_body, shape((1, 4, 8, 4096)), (pltpu.VMEM((256, 512), f32),))(
        grad_first, kern, from_above(edge)
    )
    weight_first, weight_second = call(
        final_body, (shape((4, 8, 27), f32), shape((8, 16, 27), f32))
    )(kept, swap(sent, "slab", 8))
    return (
        grad_volume,
        jnp.transpose(weight_first, (2, 0, 1)),
        jnp.transpose(weight_second, (2, 0, 1)),
    )


def solution(mesh):
    return jax.shard_map(
        on_device,
        mesh=mesh,
        in_specs=(
            P(None, "chan", "slab", None),
            P(None, "chan", "slab", None),
            P(None, "chan", "slab", None),
            P(),
            P(),
            P(None, "chan", "slab", None),
            P(None, "chan", "slab", None),
        ),
        out_specs=(P(None, "chan", "slab", None), P(None, "chan", "slab"), P(None, "chan", "slab")),
        check_vma=False,
    )
```

```python
import math

import jax
import jax.numpy as jnp
from jax import lax
from jax.experimental import pallas as pl
from jax.experimental.pallas import tpu as pltpu
from jax.sharding import PartitionSpec as P

H = 64
leaky_slope = 0.2
bf16 = jnp.bfloat16
f32 = jnp.float32
variants = ((0, 0), (0, 1), (1, 0), (1, 1))
phase_taps = (((1, 0),), ((2, 0), (0, 1)))


def index_of(shape, dim):
    return lax.broadcasted_iota(jnp.int32, shape, dim)


def rows_of(count):
    return index_of((count, 1), 0)


def lanes_of(count):
    return index_of((1, count), 1)


def one_hot(match):
    return jnp.where(match, 1.0, 0.0).astype(bf16)


def interleave_hot(log_width, to_natural):
    natural = lanes_of(512) if to_natural else rows_of(512)
    row, col = (natural >> log_width, natural & ((1 << log_width) - 1))
    source = ((row & 1) << 8) | ((col & 1) << 7) | ((row >> 1) << (log_width - 1)) | (col >> 1)
    return one_hot(source == index_of((512, 512), 0 if to_natural else 1))


def spread_hot(row_off, col_off):
    lane = lanes_of(512)
    row, col = (((lane >> 4) & 15) + row_off, (lane & 15) + col_off)
    window = ((row >> 1) << 3) + (col >> 1) + ((lane >> 8) << 6)
    window = jnp.where((row < 16) & (col < 16), window, -1)
    return one_hot(window == index_of((128, 512), 0))


def row_hot(to_grouped):
    new = rows_of(256) if to_grouped else lanes_of(256)
    source = (((new >> 3) & 7) << 5) | ((new & 3) << 3) | ((new >> 6) << 1) | ((new >> 2) & 1)
    return one_hot(source == index_of((256, 256), 1 if to_grouped else 0))


def halo_hot():
    new, old = (index_of((64, 32), 0), index_of((64, 32), 1))
    return one_hot((((new >> 3) << 2 | (new & 3)) == old) & ((new & 4) == 4))


def second_hot(row_off, col_off):
    row = rows_of(128)
    group, row_phase, col_phase = (row >> 5, (row >> 4) & 1, (row >> 3) & 1)
    depth_tap = jnp.where(group == 2, 0, group + 1)
    row_tap = 0 if row_off else 1 + row_phase
    col_tap = 0 if col_off else 1 + col_phase
    target = ((row & 7) << 5) + 9 * depth_tap + 3 * row_tap + col_tap
    valid = (group < 3) & (row_phase >= row_off) & (col_phase >= col_off)
    return one_hot(jnp.where(valid, target, -1) == index_of((128, 256), 1))


def first_hot():
    row = rows_of(128)
    tap = jnp.where(row < 72, 9 + 9 * ((row >> 2) & 1) + (row >> 3), (row - 72) >> 2)
    target = jnp.where(row < 108, ((row & 3) << 5) + tap, -1)
    return one_hot(target == index_of((128, 128), 1))


def dot(left, right):
    return jnp.dot(left, right, preferred_element_type=f32)


def dot_lanes(left, right):
    return lax.dot_general(left, right, (((1,), (1,)), ((), ())), preferred_element_type=f32)


def slope_of(values):
    return jnp.where(values > 0, 1.0, leaky_slope).astype(f32)


def cell_of(row_off, col_off):
    lane = lanes_of(256)
    cell = (((lane >> 4) + row_off) & 1) * 2 + ((lane + col_off) & 1)
    return cell.astype(f32)


def plane_of(value, plane):
    return jnp.sum(jnp.where(index_of(value.shape, 1) == plane, value, 0.0), axis=1)


def pool_body(
    pre_hbm, index_hbm, grad_hbm, first_hbm, out_ref, pre_ref, index_ref, grad_ref, first_ref, sems
):
    copies = [
        pltpu.make_async_copy(source, target, sems.at[i])
        for i, (source, target) in enumerate(
            ((first_hbm, first_ref), (pre_hbm, pre_ref), (index_hbm, index_ref), (grad_hbm, grad_ref))
        )
    ]
    for copy in copies:
        copy.start()
    cell = cell_of(0, 0)
    lane = lanes_of(256)
    spread = one_hot((((lane >> 5) << 3) | ((lane >> 1) & 7)) == index_of((64, 256), 0))
    lane = rows_of(256)
    back = one_hot((((lane >> 5) << 3) | ((lane >> 1) & 7)) == index_of((256, 128), 1))
    tag = one_hot(rows_of(64) + 64 == index_of((64, 128), 1))
    for copy in copies:
        copy.wait()
    for plane in range(4):
        out_ref[:, plane * 1024 : (plane + 1) * 1024] = first_ref[0, :, plane, :]
    index = index_ref[0, :, 0, :].astype(f32).astype(bf16)
    both = jnp.concatenate([grad_ref[...], index], 0)
    both = dot(both, spread)
    total = jnp.zeros((16, 256), f32)
    for depth in range(2):
        pre = pre_ref[0, :, depth, :].astype(f32)
        total = total + jnp.where(both[16:32] == cell + 4.0 * depth, both[0:16] * slope_of(pre), 0.0)
    small = dot(total.astype(bf16), back) + dot(index, tag)
    out_ref[:, 4096:4224] = small[0:8].astype(bf16)
    out_ref[:, 4224:4352] = small[8:16].astype(bf16)


def hold_body(kern_ref, out_ref):
    out_ref[...] = kern_ref[...]


def tap_rows(phases):
    lane = lanes_of(phases.shape[1])
    has_col = (lane & 31) > 0
    has_row = ((lane >> 5) & 31) > 0
    result = []
    for row_tap in range(3):
        row_phase = 0 if row_tap == 1 else 1
        for col_tap in range(3):
            col_phase = 0 if col_tap == 1 else 1
            phase = row_phase * 2 + col_phase
            value = phases[phase * 8 : phase * 8 + 8, :]
            if col_tap == 0:
                value = jnp.where(has_col, pltpu.roll(value, 1, 1), 0.0)
            if row_tap == 0:
                value = jnp.where(has_row, pltpu.roll(value, 32, 1), 0.0)
            result.append(value)
    return result


def below_rows(halo, out_ref, phase_buf, cols_buf):
    halo = jnp.concatenate([halo[part * 32 : (part + 1) * 32] for part in range(4)], 1)
    halo = dot(halo_hot(), dot(halo.astype(bf16), interleave_hot(6, False)).astype(bf16))
    for t in range(8):
        for phase in range(4):
            phase_buf[phase * 8 : phase * 8 + 8, t * 128 : (t + 1) * 128] = halo[
                t * 8 : t * 8 + 8, phase * 128 : (phase + 1) * 128
            ]
    cols_buf[...] = jnp.zeros_like(cols_buf)
    for tap, value in enumerate(tap_rows(phase_buf)):
        cols_buf[72 + tap * 4 : 76 + tap * 4, :] = value[4:8, :]
    out_ref[...] = cols_buf[...].astype(bf16)


def local_body(
    pre_ref, vol_ref, kern_ref,
    act_ref, act_up_ref, cols_ref, kern_out_ref, top_ref, act_buf, phase_buf, cols_buf, kern_buf, top_buf,
):
    pre = pre_ref[:, 0:4096].astype(f32)
    act = jnp.where(pre > 0, pre, leaky_slope * pre)
    stacked = jnp.concatenate([act[:, q * 512 : (q + 1) * 512] for q in range(8)], 0)
    split = dot(stacked.astype(bf16), interleave_hot(5, False))
    act_buf[...] = jnp.zeros_like(act_buf)
    for q in range(8):
        plane, half = (q // 2, q % 2)
        pair, parity = (plane // 2, plane % 2)
        for phase in range(4):
            row = (parity * 4 + phase) * 8
            lane = pair * 256 + half * 128
            piece = split[q * 8 : (q + 1) * 8, phase * 128 : (phase + 1) * 128]
            act_buf[row : row + 8, lane : lane + 128] = piece
            if parity == 1:
                row = 128 + 64 + phase * 8
                act_buf[row : row + 8, lane : lane + 128] = piece
    act_ref[...] = act_buf[0:128, :].astype(bf16)
    act_up_ref[...] = act_buf[128:256, :].astype(bf16)

    split_zero = interleave_hot(6, False)
    wide = jnp.concatenate([vol_ref[:, g * 512 : (g + 1) * 512] for g in range(8)], 0)
    ordered = dot(row_hot(True), dot(wide, split_zero).astype(bf16))
    for t in range(32):
        for phase in range(4):
            phase_buf[phase * 8 : phase * 8 + 8, t * 128 : (t + 1) * 128] = ordered[
                t * 8 : t * 8 + 8, phase * 128 : (phase + 1) * 128
            ]
    cols_buf[72:128, :] = jnp.zeros((56, 4096), f32)
    for tap, value in enumerate(tap_rows(phase_buf)):
        cols_buf[tap * 8 : tap * 8 + 8, :] = value
        cols_buf[72 + tap * 4 : 76 + tap * 4, 1024:4096] = value[4:8, 0:3072]
    cols_ref[...] = cols_buf[...].astype(bf16)
    top = plane_of(vol_ref[...].astype(f32).reshape(4, 8, 4096), 7)
    for part in range(4):
        for g in range(8):
            lane = (g * 4 + part) * 128
            top_buf[part * 32 + g * 4 : part * 32 + g * 4 + 4, :] = top[:, lane : lane + 128]
    top_ref[...] = top_buf[...].astype(bf16)

    kern_buf[...] = jnp.zeros_like(kern_buf)
    for tap in range(9):
        kern_buf[tap * 8 : tap * 8 + 4, 0:128] = kern_ref[9 + tap].astype(f32)
        kern_buf[tap * 8 + 4 : tap * 8 + 8, 0:128] = kern_ref[18 + tap].astype(f32)
        kern_buf[tap * 8 + 4 : tap * 8 + 8, 128:256] = kern_ref[tap].astype(f32)
    kern_out_ref[...] = kern_buf[...].astype(bf16)


def channel_block(col_step, row_step):
    me = lax.axis_index("chan")
    return (((me >> 2) + row_step) & 3) * 4 + (((me & 3) + col_step) & 3)


def join_small_body(m0_ref, m1_ref, m2_ref, m3_ref, after_ref, table_ref, out_ref):
    for step, ref in enumerate((m0_ref, m1_ref, m2_ref, m3_ref)):
        rows = jnp.concatenate([ref[:, 4096:4224].astype(f32), ref[:, 4224:4352].astype(f32)], 0)
        out_ref[step * 16 : step * 16 + 16, :] = rows.astype(bf16)


def join_body(m0_ref, m1_ref, m2_ref, m3_ref, out_ref):
    rows = [ref[:, 0:4096].astype(f32) for ref in (m0_ref, m1_ref, m2_ref, m3_ref)]
    out_ref[...] = jnp.concatenate(rows, 0).astype(bf16)


def order_body(s0_ref, s1_ref, s2_ref, s3_ref, top_ref, out_ref, one_ref, two_ref):
    for col_step, ref in enumerate((s0_ref, s1_ref, s2_ref, s3_ref)):
        for row_step in range(4):
            at = pl.multiple_of(channel_block(col_step, row_step) * 16, 16)
            out_ref[pl.ds(at, 16), :] = ref[row_step * 16 : row_step * 16 + 16, :]
    up = jnp.concatenate([top_ref[...].astype(f32), jnp.zeros((128, 128), f32)], 0)
    down = out_ref[...].astype(f32)
    odd = (lax.axis_index("slab") & 1).astype(f32)
    one_ref[...] = (up + odd * (down - up)).astype(bf16)
    two_ref[...] = (down + odd * (up - down)).astype(bf16)


def second_body(
    small_ref, kern_ref, act_ref, act_up_ref, grad_ref, taps_ref, grid, split
):
    small = small_ref[...]
    for v, (row_off, col_off) in enumerate(variants):
        wide = dot(small, spread_hot(row_off, col_off))
        cell = cell_of(row_off, col_off)
        for plane in range(2):
            match = wide[:, 256:512] == cell + 4.0 * plane
            grid[v, :, plane * 256 : (plane + 1) * 256] = jnp.where(
                match, wide[:, 0:256], 0.0
            ).astype(bf16)
    for v in range(4):
        taps_ref[v] = dot_lanes(grid[v], act_ref[...]) + dot_lanes(
            grid[v, :, 256:512], act_up_ref[:, 0:256]
        )
    for depth_phase in range(2):
        for row_phase in range(2):
            for col_phase in range(2):
                total = jnp.zeros((128, 512), f32)
                ahead = jnp.zeros((128, 256), f32)
                for row_tap, row_off in phase_taps[row_phase]:
                    for col_tap, col_off in phase_taps[col_phase]:
                        tap = 3 * row_tap + col_tap
                        v = row_off * 2 + col_off
                        total = total + dot(kern_ref[9 + 9 * depth_phase + tap], grid[v])
                        if depth_phase == 1:
                            ahead = ahead + dot(kern_ref[tap], grid[v, :, 256:512])
                phase = row_phase * 2 + col_phase
                for pair in range(2):
                    for half in range(2):
                        q = (2 * pair + depth_phase) * 2 + half
                        lane = pair * 256 + half * 128
                        piece = total[:, lane : lane + 128]
                        if pair == 0 and depth_phase == 1:
                            piece = piece + ahead[:, lane : lane + 128]
                        put_split(split, q, phase, piece)
    put_natural(split, grad_ref, 8)


def put_split(split, q, phase, piece):
    rounded = piece.astype(bf16)
    rows = slice(q * 128, (q + 1) * 128)
    split[rows, phase * 128 : (phase + 1) * 128] = rounded
    split[rows, 512 + phase * 128 : 512 + (phase + 1) * 128] = (piece - rounded.astype(f32)).astype(bf16)


def put_natural(split, grad_ref, count):
    inter = interleave_hot(5, True)
    natural = dot(split[...], jnp.concatenate([inter, inter], 0))
    for q in range(count):
        grad_ref[:, q * 512 : (q + 1) * 512] = natural[q * 128 : (q + 1) * 128, :]


def second_halo_body(
    one_ref, two_ref, kern_ref, act_up_ref, taps_in_ref,
    grad_ref, taps_ref, below_ref, split, phase_buf, cols_buf,
):
    one, two = (one_ref[...].astype(f32), two_ref[...].astype(f32))
    odd = (lax.axis_index("slab") & 1).astype(f32)
    above = (one + odd * (two - one)).astype(bf16)
    below_rows((two + odd * (one - two))[0:128], below_ref, phase_buf, cols_buf)
    grid, parts = ([], [])
    for v, (row_off, col_off) in enumerate(variants):
        wide = dot(above, spread_hot(row_off, col_off))
        match = wide[:, 256:512] == cell_of(row_off, col_off)
        grid.append(jnp.where(match, wide[:, 0:256], 0.0).astype(bf16))
        part = taps_in_ref[v] + dot_lanes(grid[v], act_up_ref[:, 256:512])
        parts.append(part.astype(bf16))
    select = jnp.concatenate([second_hot(*variant) for variant in variants], 0)
    taps_ref[...] = dot(jnp.concatenate(parts, 1), select).astype(bf16)
    for row_phase in range(2):
        for col_phase in range(2):
            taps = [
                (3 * row_tap + col_tap, row_off * 2 + col_off)
                for row_tap, row_off in phase_taps[row_phase]
                for col_tap, col_off in phase_taps[col_phase]
            ]
            total = dot(
                jnp.concatenate([kern_ref[tap] for tap, _ in taps], 1),
                jnp.concatenate([grid[v] for _, v in taps], 0),
            )
            for half in range(2):
                put_split(split, half, row_phase * 2 + col_phase, total[:, half * 128 : half * 128 + 128])
    put_natural(split, grad_ref, 2)


def next_col(value):
    lane = lanes_of(value.shape[1])
    return jnp.where((lane & 31) < 31, pltpu.roll(value, value.shape[1] - 1, 1), 0.0)


def next_row(value):
    lane = lanes_of(value.shape[1])
    return jnp.where(((lane >> 5) & 31) < 31, pltpu.roll(value, value.shape[1] - 32, 1), 0.0)


def fold_taps(wide):
    def group(row_tap, col_tap):
        at = (row_tap * 3 + col_tap) * 8
        return wide[at : at + 8, :]

    return (
        group(1, 1),
        group(1, 2) + next_col(group(1, 0)),
        group(2, 1) + next_row(group(0, 1)),
        group(2, 2) + next_col(group(2, 0)) + next_row(group(0, 2) + next_col(group(0, 0))),
    )


def first_taps_body(
    p0_ref, p1_ref, p2_ref, p3_ref, grad_ref, halo_ref, cols_ref, below_ref, second_ref,
    first_ref, kept_ref, sent_ref, buf, taps_buf,
):
    for col_step, ref in enumerate((p0_ref, p1_ref, p2_ref, p3_ref)):
        slope = slope_of(ref[...].astype(f32))
        for row_step in range(4):
            at = pl.multiple_of(channel_block(col_step, row_step) * 8, 8)
            rows = slope[row_step * 8 : (row_step + 1) * 8, :]
            buf[pl.ds(at, 8), 0:3072] = grad_ref[pl.ds(at, 8), 0:3072] * rows[:, 0:3072]
            last = grad_ref[pl.ds(at, 8), 3072:4096] + halo_ref[pl.ds(at, 8), :]
            buf[pl.ds(at, 8), 3072:4096] = last * rows[:, 3072:4096]
    first_ref[...] = buf[...].astype(bf16)
    taps = dot_lanes(first_ref[...], cols_ref[...])
    taps = (taps + dot_lanes(first_ref[:, 0:1024], below_ref[...])).astype(bf16)
    taps_buf[...] = dot(taps, first_hot())
    core = lax.axis_index("slab") & 1
    for pair in range(8):
        for ref, which in ((kept_ref, core), (sent_ref, 1 - core)):
            slab = pair * 2 + which
            ref[pair, :, 0:256] = second_ref[pl.ds(pl.multiple_of(slab * 16, 16), 16), :]
            part = taps_buf[pl.ds(pl.multiple_of(slab * 8, 8), 8), :]
            ref[pair, :, 256:384] = jnp.concatenate([part, jnp.zeros((8, 128), f32)], 0).astype(bf16)


def edge_body(first_ref, kern_ref, out_ref):
    edges = fold_taps(dot(kern_ref[:, 128:256], first_ref[:, 0:1024]))
    out_ref[...] = jnp.concatenate([edge[4:8, :] for edge in edges], 0).astype(bf16)


def first_body(first_ref, kern_ref, edge_ref, out_ref, buf):
    ahead = dot(kern_ref[:, 128:256], first_ref[:, 1024:4096])
    ahead = jnp.concatenate([ahead, jnp.zeros((72, 1024), f32)], 1)
    phases = fold_taps(dot(kern_ref[:, 0:128], first_ref[...]) + ahead)
    edge = edge_ref[...].astype(f32)
    for t in range(32):
        for phase in range(4):
            value = phases[phase][:, t * 128 : (t + 1) * 128]
            if t >= 24:
                lane = (t - 24) * 128
                extra = edge[phase * 4 : (phase + 1) * 4, lane : lane + 128]
                value = value + jnp.concatenate([jnp.zeros((4, 128), f32), extra], 0)
            buf[t * 8 : (t + 1) * 8, phase * 128 : (phase + 1) * 128] = value
    ordered = dot(row_hot(False), buf[...].astype(bf16)).astype(bf16)
    natural = dot(ordered, interleave_hot(6, True))
    for g in range(8):
        for channel in range(4):
            at = g * 32 + channel * 8
            out_ref[0, channel, :, g * 512 : (g + 1) * 512] = natural[at : at + 8, :].astype(bf16)


def middle_body(kept_ref, came_ref, edge_ref, next_ref, s1_ref, s2_ref, s3_ref):
    y = (lax.axis_index("slab") >> 1) & 3
    for z in range(2):
        for step, ref in enumerate((next_ref, s1_ref, s2_ref, s3_ref)):
            at = z * 4 + ((y + step) & 3)
            value = kept_ref[at].astype(f32) + came_ref[at].astype(f32)
            ref[z] = value.astype(ref.dtype)


def late_body(kept_ref, c1_ref, c2_ref, c3_ref, next_ref, sent_ref):
    z = lax.axis_index("slab") >> 3

    def total(at):
        value = kept_ref[at]
        for ref in (c1_ref, c2_ref, c3_ref):
            value = value + ref[at].astype(f32)
        return value

    next_ref[...] = total(z)
    sent_ref[...] = total(1 - z).astype(bf16)


def final_body(kept_ref, came_ref, first_ref, second_ref):
    total = kept_ref[...] + came_ref[...].astype(f32)
    for channel in range(8):
        at = channel * 32
        second_ref[channel] = total[:, at : at + 27] * (1.0 / math.sqrt(1024.0))
    for channel in range(4):
        at = 256 + channel * 32
        first_ref[channel] = total[0:8, at : at + 27] * (1.0 / math.sqrt(65536.0))


def call(body, out, scratch=(), micros=0.05, limit=16, **options):
    return pl.pallas_call(
        body,
        out_shape=out,
        scratch_shapes=list(scratch),
        compiler_params=pltpu.CompilerParams(vmem_limit_bytes=limit * 1024 * 1024),
        cost_estimate=pl.CostEstimate(
            flops=int(micros * 1.0e9), bytes_accessed=100000, transcendentals=0
        ),
        **options,
    )


def shape(dims, dtype=bf16):
    return jax.ShapeDtypeStruct(dims, dtype)


def from_ahead_x(value, step):
    return lax.ppermute(
        value, "chan", [((s // 4) * 4 + (s % 4 + step) % 4, s) for s in range(16)]
    )


def from_ahead_z(value, step):
    return lax.ppermute(value, "chan", [((s + 4 * step) % 16, s) for s in range(16)])


def gather(value, exchange):
    came = {step: exchange(value, step) for step in (1, 2, 3)}
    return [value, came[1], came[2], came[3]]


def from_above(value):
    return lax.ppermute(value, "slab", [(s, s - 1) for s in range(1, 16)])


def swap_next(value):
    pairs = [(s, s + 1) for s in range(1, 14, 2)] + [(s + 1, s) for s in range(1, 14, 2)]
    return lax.ppermute(value, "slab", pairs)


def swap(value, axis, mask):
    return lax.ppermute(value, axis, [(s, s ^ mask) for s in range(16)])


def on_device(
    volume_in, pre_first, pre_second, kernel_first, kernel_second, pool_index, grad_pooled
):
    message = call(
        pool_body,
        shape((8, 4352)),
        (
            pltpu.VMEM((1, 16, 2, 256), bf16),
            pltpu.VMEM((1, 16, 1, 64), jnp.int32),
            pltpu.VMEM((16, 64), bf16),
            pltpu.VMEM((1, 8, 4, 1024), bf16),
            pltpu.SemaphoreType.DMA((4,)),
        ),
        limit=60,
        in_specs=[pl.BlockSpec(memory_space=pltpu.HBM)] * 4,
    )(pre_second, pool_index, grad_pooled.reshape(16, 64), pre_first)
    kernel_second = call(hold_body, shape((27, 128, 256)))(kernel_second)
    own_kernel = lax.dynamic_slice_in_dim(kernel_first, lax.axis_index("chan") * 4, 4, 1)
    act, act_up, cols, kern, top = call(
        local_body,
        (shape((128, 512)), shape((128, 512)), shape((128, 4096)), shape((72, 256)), shape((128, 128))),
        (
            pltpu.VMEM((256, 512), f32),
            pltpu.VMEM((32, 4096), f32),
            pltpu.VMEM((128, 4096), f32),
            pltpu.VMEM((72, 256), f32),
            pltpu.VMEM((128, 128), f32),
        ),
    )(message, volume_in.reshape(32, 4096), own_kernel)

    whole = pl.BlockSpec(memory_space=pltpu.VMEM)
    unread = pl.BlockSpec(memory_space=pl.ANY)
    messages = gather(message, from_ahead_z)
    small = call(join_small_body, shape((64, 128)), in_specs=[whole] * 4 + [unread] * 2)(
        *messages, top, kernel_second
    )
    block = (256, 128)
    small, one, two = call(order_body, (shape(block), shape(block), shape(block)))(
        *gather(small, from_ahead_x), top
    )
    pre_all = gather(call(join_body, shape((32, 4096)))(*messages), from_ahead_x)
    one, two = (swap(one, "slab", 1), swap_next(two))
    grad_act, second = call(
        second_body,
        (shape((128, 4096), f32), shape((4, 256, 128), f32)),
        (pltpu.VMEM((4, 256, 512), bf16), pltpu.VMEM((1024, 1024), bf16)),
        micros=3.0,
    )(small, kernel_second, act, act_up)
    grad_halo, second, below = call(
        second_halo_body,
        (shape((128, 1024), f32), shape((256, 256)), shape((128, 1024))),
        (
            pltpu.VMEM((256, 1024), bf16),
            pltpu.VMEM((32, 1024), f32),
            pltpu.VMEM((128, 1024), f32),
        ),
        micros=2.0,
    )(one, two, kernel_second, act_up, second)
    grad_first, kept, sent = call(
        first_taps_body,
        (shape((128, 4096)), shape((8, 16, 384)), shape((8, 16, 384))),
        (pltpu.VMEM((128, 4096), f32), pltpu.VMEM((128, 128), f32)),
    )(*pre_all, grad_act, grad_halo, cols, below, second)
    edge = call(edge_body, shape((16, 1024)))(grad_first, kern)

    block = (2, 16, 384)
    kept, *sent = call(
        middle_body,
        (shape(block, f32), shape(block), shape(block), shape(block)),
        in_specs=[whole, whole, unread],
    )(kept, swap(sent, "slab", 1), edge)
    came = []
    for step in (1, 2, 3):
        pairs = [(s, (s & 9) | ((((s >> 1) + step) & 3) << 1)) for s in range(16)]
        came.append(lax.ppermute(sent[step - 1], "slab", pairs))
    kept, sent = call(late_body, (shape((16, 384), f32), shape((16, 384))))(kept, *came)
    grad_volume = call(first_body, shape((1, 4, 8, 4096)), (pltpu.VMEM((256, 512), f32),))(
        grad_first, kern, from_above(edge)
    )
    weight_first, weight_second = call(
        final_body, (shape((4, 8, 27), f32), shape((8, 16, 27), f32))
    )(kept, swap(sent, "slab", 8))
    return (
        grad_volume,
        jnp.transpose(weight_first, (2, 0, 1)),
        jnp.transpose(weight_second, (2, 0, 1)),
    )


def solution(mesh):
    return jax.shard_map(
        on_device,
        mesh=mesh,
        in_specs=(
            P(None, "chan", "slab", None),
            P(None, "chan", "slab", None),
            P(None, "chan", "slab", None),
            P(),
            P(),
            P(None, "chan", "slab", None),
            P(None, "chan", "slab", None),
        ),
        out_specs=(P(None, "chan", "slab", None), P(None, "chan", "slab"), P(None, "chan", "slab")),
        check_vma=False,
    )
```

```python
import math

import jax
import jax.numpy as jnp
from jax import lax
from jax.experimental import pallas as pl
from jax.experimental.pallas import tpu as pltpu
from jax.sharding import PartitionSpec as P

H = 64
leaky_slope = 0.2
bf16 = jnp.bfloat16
f32 = jnp.float32
variants = ((0, 0), (0, 1), (1, 0), (1, 1))
phase_taps = (((1, 0),), ((2, 0), (0, 1)))


def index_of(shape, dim):
    return lax.broadcasted_iota(jnp.int32, shape, dim)


def rows_of(count):
    return index_of((count, 1), 0)


def lanes_of(count):
    return index_of((1, count), 1)


def one_hot(match):
    return jnp.where(match, 1.0, 0.0).astype(bf16)


def interleave_hot(log_width, to_natural):
    natural = lanes_of(512) if to_natural else rows_of(512)
    row, col = (natural >> log_width, natural & ((1 << log_width) - 1))
    source = ((row & 1) << 8) | ((col & 1) << 7) | ((row >> 1) << (log_width - 1)) | (col >> 1)
    return one_hot(source == index_of((512, 512), 0 if to_natural else 1))


def spread_hot(row_off, col_off):
    lane = lanes_of(512)
    row, col = (((lane >> 4) & 15) + row_off, (lane & 15) + col_off)
    window = ((row >> 1) << 3) + (col >> 1) + ((lane >> 8) << 6)
    window = jnp.where((row < 16) & (col < 16), window, -1)
    return one_hot(window == index_of((128, 512), 0))


def row_hot(to_grouped):
    new = rows_of(256) if to_grouped else lanes_of(256)
    source = (((new >> 3) & 7) << 5) | ((new & 3) << 3) | ((new >> 6) << 1) | ((new >> 2) & 1)
    return one_hot(source == index_of((256, 256), 1 if to_grouped else 0))


def halo_hot():
    new, old = (index_of((64, 32), 0), index_of((64, 32), 1))
    return one_hot((((new >> 3) << 2 | (new & 3)) == old) & ((new & 4) == 4))


def second_hot(row_off, col_off):
    row = rows_of(128)
    group, row_phase, col_phase = (row >> 5, (row >> 4) & 1, (row >> 3) & 1)
    depth_tap = jnp.where(group == 2, 0, group + 1)
    row_tap = 0 if row_off else 1 + row_phase
    col_tap = 0 if col_off else 1 + col_phase
    target = ((row & 7) << 5) + 9 * depth_tap + 3 * row_tap + col_tap
    valid = (group < 3) & (row_phase >= row_off) & (col_phase >= col_off)
    return one_hot(jnp.where(valid, target, -1) == index_of((128, 256), 1))


def first_hot():
    row = rows_of(128)
    tap = jnp.where(row < 72, 9 + 9 * ((row >> 2) & 1) + (row >> 3), (row - 72) >> 2)
    target = jnp.where(row < 108, ((row & 3) << 5) + tap, -1)
    return one_hot(target == index_of((128, 128), 1))


def dot(left, right):
    return jnp.dot(left, right, preferred_element_type=f32)


def dot_lanes(left, right):
    return lax.dot_general(left, right, (((1,), (1,)), ((), ())), preferred_element_type=f32)


def slope_of(values):
    return jnp.where(values > 0, 1.0, leaky_slope).astype(f32)


def cell_of(row_off, col_off):
    lane = lanes_of(256)
    cell = (((lane >> 4) + row_off) & 1) * 2 + ((lane + col_off) & 1)
    return cell.astype(f32)


def plane_of(value, plane):
    return jnp.sum(jnp.where(index_of(value.shape, 1) == plane, value, 0.0), axis=1)


def pool_body(
    pre_hbm, index_hbm, grad_hbm, first_hbm, out_ref, pre_ref, index_ref, grad_ref, first_ref, sems
):
    copies = [
        pltpu.make_async_copy(source, target, sems.at[i])
        for i, (source, target) in enumerate(
            ((first_hbm, first_ref), (pre_hbm, pre_ref), (index_hbm, index_ref), (grad_hbm, grad_ref))
        )
    ]
    for copy in copies:
        copy.start()
    cell = cell_of(0, 0)
    lane = lanes_of(256)
    spread = one_hot((((lane >> 5) << 3) | ((lane >> 1) & 7)) == index_of((64, 256), 0))
    lane = rows_of(256)
    back = one_hot((((lane >> 5) << 3) | ((lane >> 1) & 7)) == index_of((256, 128), 1))
    tag = one_hot(rows_of(64) + 64 == index_of((64, 128), 1))
    for copy in copies:
        copy.wait()
    for plane in range(4):
        out_ref[:, plane * 1024 : (plane + 1) * 1024] = first_ref[0, :, plane, :]
    index = index_ref[0, :, 0, :].astype(f32).astype(bf16)
    both = jnp.concatenate([grad_ref[...], index], 0)
    both = dot(both, spread)
    total = jnp.zeros((16, 256), f32)
    for depth in range(2):
        pre = pre_ref[0, :, depth, :].astype(f32)
        total = total + jnp.where(both[16:32] == cell + 4.0 * depth, both[0:16] * slope_of(pre), 0.0)
    small = dot(total.astype(bf16), back) + dot(index, tag)
    out_ref[:, 4096:4224] = small[0:8].astype(bf16)
    out_ref[:, 4224:4352] = small[8:16].astype(bf16)


def hold_body(kern_ref, out_ref):
    out_ref[...] = kern_ref[...]


def tap_rows(phases):
    lane = lanes_of(phases.shape[1])
    has_col = (lane & 31) > 0
    has_row = ((lane >> 5) & 31) > 0
    result = []
    for row_tap in range(3):
        row_phase = 0 if row_tap == 1 else 1
        for col_tap in range(3):
            col_phase = 0 if col_tap == 1 else 1
            phase = row_phase * 2 + col_phase
            value = phases[phase * 8 : phase * 8 + 8, :]
            if col_tap == 0:
                value = jnp.where(has_col, pltpu.roll(value, 1, 1), 0.0)
            if row_tap == 0:
                value = jnp.where(has_row, pltpu.roll(value, 32, 1), 0.0)
            result.append(value)
    return result


def below_rows(halo, out_ref, phase_buf, cols_buf):
    halo = jnp.concatenate([halo[part * 32 : (part + 1) * 32] for part in range(4)], 1)
    halo = dot(halo_hot(), dot(halo.astype(bf16), interleave_hot(6, False)).astype(bf16))
    for t in range(8):
        for phase in range(4):
            phase_buf[phase * 8 : phase * 8 + 8, t * 128 : (t + 1) * 128] = halo[
                t * 8 : t * 8 + 8, phase * 128 : (phase + 1) * 128
            ]
    cols_buf[...] = jnp.zeros_like(cols_buf)
    for tap, value in enumerate(tap_rows(phase_buf)):
        cols_buf[72 + tap * 4 : 76 + tap * 4, :] = value[4:8, :]
    out_ref[...] = cols_buf[...].astype(bf16)


def local_body(
    pre_ref, vol_ref, kern_ref,
    act_ref, act_up_ref, cols_ref, kern_out_ref, top_ref, act_buf, phase_buf, cols_buf, kern_buf, top_buf,
):
    pre = pre_ref[:, 0:4096].astype(f32)
    act = jnp.where(pre > 0, pre, leaky_slope * pre)
    stacked = jnp.concatenate([act[:, q * 512 : (q + 1) * 512] for q in range(8)], 0)
    split = dot(stacked.astype(bf16), interleave_hot(5, False))
    act_buf[...] = jnp.zeros_like(act_buf)
    for q in range(8):
        plane, half = (q // 2, q % 2)
        pair, parity = (plane // 2, plane % 2)
        for phase in range(4):
            row = (parity * 4 + phase) * 8
            lane = pair * 256 + half * 128
            piece = split[q * 8 : (q + 1) * 8, phase * 128 : (phase + 1) * 128]
            act_buf[row : row + 8, lane : lane + 128] = piece
            if parity == 1:
                row = 128 + 64 + phase * 8
                act_buf[row : row + 8, lane : lane + 128] = piece
    act_ref[...] = act_buf[0:128, :].astype(bf16)
    act_up_ref[...] = act_buf[128:256, :].astype(bf16)

    split_zero = interleave_hot(6, False)
    wide = jnp.concatenate([vol_ref[:, g * 512 : (g + 1) * 512] for g in range(8)], 0)
    ordered = dot(row_hot(True), dot(wide, split_zero).astype(bf16))
    for t in range(32):
        for phase in range(4):
            phase_buf[phase * 8 : phase * 8 + 8, t * 128 : (t + 1) * 128] = ordered[
                t * 8 : t * 8 + 8, phase * 128 : (phase + 1) * 128
            ]
    cols_buf[72:128, :] = jnp.zeros((56, 4096), f32)
    for tap, value in enumerate(tap_rows(phase_buf)):
        cols_buf[tap * 8 : tap * 8 + 8, :] = value
        cols_buf[72 + tap * 4 : 76 + tap * 4, 1024:4096] = value[4:8, 0:3072]
    cols_ref[...] = cols_buf[...].astype(bf16)
    top = plane_of(vol_ref[...].astype(f32).reshape(4, 8, 4096), 7)
    for part in range(4):
        for g in range(8):
            lane = (g * 4 + part) * 128
            top_buf[part * 32 + g * 4 : part * 32 + g * 4 + 4, :] = top[:, lane : lane + 128]
    top_ref[...] = top_buf[...].astype(bf16)

    kern_buf[...] = jnp.zeros_like(kern_buf)
    for tap in range(9):
        kern_buf[tap * 8 : tap * 8 + 4, 0:128] = kern_ref[9 + tap].astype(f32)
        kern_buf[tap * 8 + 4 : tap * 8 + 8, 0:128] = kern_ref[18 + tap].astype(f32)
        kern_buf[tap * 8 + 4 : tap * 8 + 8, 128:256] = kern_ref[tap].astype(f32)
    kern_out_ref[...] = kern_buf[...].astype(bf16)


def channel_block(col_step, row_step):
    me = lax.axis_index("chan")
    return (((me >> 2) + row_step) & 3) * 4 + (((me & 3) + col_step) & 3)


def join_small_body(m0_ref, m1_ref, m2_ref, m3_ref, after_ref, table_ref, out_ref):
    for step, ref in enumerate((m0_ref, m1_ref, m2_ref, m3_ref)):
        rows = jnp.concatenate([ref[:, 4096:4224].astype(f32), ref[:, 4224:4352].astype(f32)], 0)
        out_ref[step * 16 : step * 16 + 16, :] = rows.astype(bf16)


def join_body(m0_ref, m1_ref, m2_ref, m3_ref, out_ref):
    rows = [ref[:, 0:4096].astype(f32) for ref in (m0_ref, m1_ref, m2_ref, m3_ref)]
    out_ref[...] = jnp.concatenate(rows, 0).astype(bf16)


def order_body(s0_ref, s1_ref, s2_ref, s3_ref, top_ref, out_ref, one_ref, two_ref):
    for col_step, ref in enumerate((s0_ref, s1_ref, s2_ref, s3_ref)):
        for row_step in range(4):
            at = pl.multiple_of(channel_block(col_step, row_step) * 16, 16)
            out_ref[pl.ds(at, 16), :] = ref[row_step * 16 : row_step * 16 + 16, :]
    up = jnp.concatenate([top_ref[...].astype(f32), jnp.zeros((128, 128), f32)], 0)
    down = out_ref[...].astype(f32)
    odd = (lax.axis_index("slab") & 1).astype(f32)
    one_ref[...] = (up + odd * (down - up)).astype(bf16)
    two_ref[...] = (down + odd * (up - down)).astype(bf16)


def second_body(
    small_ref, kern_ref, act_ref, act_up_ref, grad_ref, taps_ref, grid, phases
):
    small = small_ref[...]
    for v, (row_off, col_off) in enumerate(variants):
        wide = dot(small, spread_hot(row_off, col_off))
        cell = cell_of(row_off, col_off)
        for plane in range(2):
            match = wide[:, 256:512] == cell + 4.0 * plane
            grid[v, :, plane * 256 : (plane + 1) * 256] = jnp.where(
                match, wide[:, 0:256], 0.0
            ).astype(bf16)
    for v in range(4):
        taps_ref[v] = dot_lanes(grid[v], act_ref[...]) + dot_lanes(
            grid[v, :, 256:512], act_up_ref[:, 0:256]
        )
    for depth_phase in range(2):
        for row_phase in range(2):
            for col_phase in range(2):
                total = jnp.zeros((128, 512), f32)
                ahead = jnp.zeros((128, 256), f32)
                for row_tap, row_off in phase_taps[row_phase]:
                    for col_tap, col_off in phase_taps[col_phase]:
                        tap = 3 * row_tap + col_tap
                        v = row_off * 2 + col_off
                        total = total + dot(kern_ref[9 + 9 * depth_phase + tap], grid[v])
                        if depth_phase == 1:
                            ahead = ahead + dot(kern_ref[tap], grid[v, :, 256:512])
                phase = row_phase * 2 + col_phase
                for pair in range(2):
                    for half in range(2):
                        q = (2 * pair + depth_phase) * 2 + half
                        lane = pair * 256 + half * 128
                        piece = total[:, lane : lane + 128]
                        if pair == 0 and depth_phase == 1:
                            piece = piece + ahead[:, lane : lane + 128]
                        phases[q * 128 : (q + 1) * 128, phase * 128 : (phase + 1) * 128] = piece.astype(bf16)
    put_natural(phases, grad_ref, 8)


def put_split(split, q, phase, piece):
    rounded = piece.astype(bf16)
    rows = slice(q * 128, (q + 1) * 128)
    split[rows, phase * 128 : (phase + 1) * 128] = rounded
    split[rows, 512 + phase * 128 : 512 + (phase + 1) * 128] = (piece - rounded.astype(f32)).astype(bf16)


def put_natural(split, grad_ref, count):
    inter = interleave_hot(5, True)
    if split.shape[1] == 1024:
        inter = jnp.concatenate([inter, inter], 0)
    natural = dot(split[...], inter)
    for q in range(count):
        grad_ref[:, q * 512 : (q + 1) * 512] = natural[q * 128 : (q + 1) * 128, :]


def second_halo_body(
    one_ref, two_ref, kern_ref, act_up_ref, taps_in_ref,
    grad_ref, taps_ref, below_ref, split, phase_buf, cols_buf,
):
    one, two = (one_ref[...].astype(f32), two_ref[...].astype(f32))
    odd = (lax.axis_index("slab") & 1).astype(f32)
    above = (one + odd * (two - one)).astype(bf16)
    below_rows((two + odd * (one - two))[0:128], below_ref, phase_buf, cols_buf)
    grid, parts = ([], [])
    for v, (row_off, col_off) in enumerate(variants):
        wide = dot(above, spread_hot(row_off, col_off))
        match = wide[:, 256:512] == cell_of(row_off, col_off)
        grid.append(jnp.where(match, wide[:, 0:256], 0.0).astype(bf16))
        part = taps_in_ref[v] + dot_lanes(grid[v], act_up_ref[:, 256:512])
        parts.append(part.astype(bf16))
    select = jnp.concatenate([second_hot(*variant) for variant in variants], 0)
    taps_ref[...] = dot(jnp.concatenate(parts, 1), select).astype(bf16)
    for row_phase in range(2):
        for col_phase in range(2):
            total = jnp.zeros((128, 256), f32)
            for row_tap, row_off in phase_taps[row_phase]:
                for col_tap, col_off in phase_taps[col_phase]:
                    total = total + dot(kern_ref[3 * row_tap + col_tap], grid[row_off * 2 + col_off])
            for half in range(2):
                put_split(split, half, row_phase * 2 + col_phase, total[:, half * 128 : half * 128 + 128])
    put_natural(split, grad_ref, 2)


def next_col(value):
    lane = lanes_of(value.shape[1])
    return jnp.where((lane & 31) < 31, pltpu.roll(value, value.shape[1] - 1, 1), 0.0)


def next_row(value):
    lane = lanes_of(value.shape[1])
    return jnp.where(((lane >> 5) & 31) < 31, pltpu.roll(value, value.shape[1] - 32, 1), 0.0)


def fold_taps(wide):
    def group(row_tap, col_tap):
        at = (row_tap * 3 + col_tap) * 8
        return wide[at : at + 8, :]

    return (
        group(1, 1),
        group(1, 2) + next_col(group(1, 0)),
        group(2, 1) + next_row(group(0, 1)),
        group(2, 2) + next_col(group(2, 0)) + next_row(group(0, 2) + next_col(group(0, 0))),
    )


def first_taps_body(
    p0_ref, p1_ref, p2_ref, p3_ref, grad_ref, halo_ref, cols_ref, below_ref, second_ref,
    first_ref, kept_ref, sent_ref, buf, taps_buf,
):
    for col_step, ref in enumerate((p0_ref, p1_ref, p2_ref, p3_ref)):
        slope = slope_of(ref[...].astype(f32))
        for row_step in range(4):
            at = pl.multiple_of(channel_block(col_step, row_step) * 8, 8)
            rows = slope[row_step * 8 : (row_step + 1) * 8, :]
            buf[pl.ds(at, 8), 0:3072] = grad_ref[pl.ds(at, 8), 0:3072] * rows[:, 0:3072]
            last = grad_ref[pl.ds(at, 8), 3072:4096] + halo_ref[pl.ds(at, 8), :]
            buf[pl.ds(at, 8), 3072:4096] = last * rows[:, 3072:4096]
    first_ref[...] = buf[...].astype(bf16)
    taps = dot_lanes(first_ref[...], cols_ref[...])
    taps = (taps + dot_lanes(first_ref[:, 0:1024], below_ref[...])).astype(bf16)
    taps_buf[...] = dot(taps, first_hot())
    core = lax.axis_index("slab") & 1
    for pair in range(8):
        for ref, which in ((kept_ref, core), (sent_ref, 1 - core)):
            slab = pair * 2 + which
            ref[pair, :, 0:256] = second_ref[pl.ds(pl.multiple_of(slab * 16, 16), 16), :]
            part = taps_buf[pl.ds(pl.multiple_of(slab * 8, 8), 8), :]
            ref[pair, :, 256:384] = jnp.concatenate([part, jnp.zeros((8, 128), f32)], 0).astype(bf16)


def edge_body(first_ref, kern_ref, out_ref):
    edges = fold_taps(dot(kern_ref[:, 128:256], first_ref[:, 0:1024]))
    out_ref[...] = jnp.concatenate([edge[4:8, :] for edge in edges], 0).astype(bf16)


def first_body(first_ref, kern_ref, edge_ref, out_ref, buf):
    ahead = dot(kern_ref[:, 128:256], first_ref[:, 1024:4096])
    ahead = jnp.concatenate([ahead, jnp.zeros((72, 1024), f32)], 1)
    phases = fold_taps(dot(kern_ref[:, 0:128], first_ref[...]) + ahead)
    edge = edge_ref[...].astype(f32)
    for t in range(32):
        for phase in range(4):
            value = phases[phase][:, t * 128 : (t + 1) * 128]
            if t >= 24:
                lane = (t - 24) * 128
                extra = edge[phase * 4 : (phase + 1) * 4, lane : lane + 128]
                value = value + jnp.concatenate([jnp.zeros((4, 128), f32), extra], 0)
            buf[t * 8 : (t + 1) * 8, phase * 128 : (phase + 1) * 128] = value
    ordered = dot(row_hot(False), buf[...].astype(bf16)).astype(bf16)
    natural = dot(ordered, interleave_hot(6, True))
    for g in range(8):
        for channel in range(4):
            at = g * 32 + channel * 8
            out_ref[0, channel, :, g * 512 : (g + 1) * 512] = natural[at : at + 8, :].astype(bf16)


def middle_body(kept_ref, came_ref, edge_ref, next_ref, s1_ref, s2_ref, s3_ref):
    y = (lax.axis_index("slab") >> 1) & 3
    for z in range(2):
        for step, ref in enumerate((next_ref, s1_ref, s2_ref, s3_ref)):
            at = z * 4 + ((y + step) & 3)
            value = kept_ref[at].astype(f32) + came_ref[at].astype(f32)
            ref[z] = value.astype(ref.dtype)


def late_body(kept_ref, c1_ref, c2_ref, c3_ref, next_ref, sent_ref):
    z = lax.axis_index("slab") >> 3

    def total(at):
        value = kept_ref[at]
        for ref in (c1_ref, c2_ref, c3_ref):
            value = value + ref[at].astype(f32)
        return value

    next_ref[...] = total(z)
    sent_ref[...] = total(1 - z).astype(bf16)


def final_body(kept_ref, came_ref, first_ref, second_ref):
    total = kept_ref[...] + came_ref[...].astype(f32)
    for channel in range(8):
        at = channel * 32
        second_ref[channel] = total[:, at : at + 27] * (1.0 / math.sqrt(1024.0))
    for channel in range(4):
        at = 256 + channel * 32
        first_ref[channel] = total[0:8, at : at + 27] * (1.0 / math.sqrt(65536.0))


def call(body, out, scratch=(), micros=0.05, limit=16, **options):
    return pl.pallas_call(
        body,
        out_shape=out,
        scratch_shapes=list(scratch),
        compiler_params=pltpu.CompilerParams(vmem_limit_bytes=limit * 1024 * 1024),
        cost_estimate=pl.CostEstimate(
            flops=int(micros * 1.0e9), bytes_accessed=100000, transcendentals=0
        ),
        **options,
    )


def shape(dims, dtype=bf16):
    return jax.ShapeDtypeStruct(dims, dtype)


def from_ahead_x(value, step):
    return lax.ppermute(
        value, "chan", [((s // 4) * 4 + (s % 4 + step) % 4, s) for s in range(16)]
    )


def from_ahead_z(value, step):
    return lax.ppermute(value, "chan", [((s + 4 * step) % 16, s) for s in range(16)])


def gather(value, exchange):
    came = {step: exchange(value, step) for step in (1, 2, 3)}
    return [value, came[1], came[2], came[3]]


def from_above(value):
    return lax.ppermute(value, "slab", [(s, s - 1) for s in range(1, 16)])


def swap_next(value):
    pairs = [(s, s + 1) for s in range(1, 14, 2)] + [(s + 1, s) for s in range(1, 14, 2)]
    return lax.ppermute(value, "slab", pairs)


def swap(value, axis, mask):
    return lax.ppermute(value, axis, [(s, s ^ mask) for s in range(16)])


def on_device(
    volume_in, pre_first, pre_second, kernel_first, kernel_second, pool_index, grad_pooled
):
    message = call(
        pool_body,
        shape((8, 4352)),
        (
            pltpu.VMEM((1, 16, 2, 256), bf16),
            pltpu.VMEM((1, 16, 1, 64), jnp.int32),
            pltpu.VMEM((16, 64), bf16),
            pltpu.VMEM((1, 8, 4, 1024), bf16),
            pltpu.SemaphoreType.DMA((4,)),
        ),
        limit=60,
        in_specs=[pl.BlockSpec(memory_space=pltpu.HBM)] * 4,
    )(pre_second, pool_index, grad_pooled.reshape(16, 64), pre_first)
    kernel_second = call(hold_body, shape((27, 128, 256)))(kernel_second)
    own_kernel = lax.dynamic_slice_in_dim(kernel_first, lax.axis_index("chan") * 4, 4, 1)
    act, act_up, cols, kern, top = call(
        local_body,
        (shape((128, 512)), shape((128, 512)), shape((128, 4096)), shape((72, 256)), shape((128, 128))),
        (
            pltpu.VMEM((256, 512), f32),
            pltpu.VMEM((32, 4096), f32),
            pltpu.VMEM((128, 4096), f32),
            pltpu.VMEM((72, 256), f32),
            pltpu.VMEM((128, 128), f32),
        ),
    )(message, volume_in.reshape(32, 4096), own_kernel)

    whole = pl.BlockSpec(memory_space=pltpu.VMEM)
    unread = pl.BlockSpec(memory_space=pl.ANY)
    messages = gather(message, from_ahead_z)
    small = call(join_small_body, shape((64, 128)), in_specs=[whole] * 4 + [unread] * 2)(
        *messages, top, kernel_second
    )
    block = (256, 128)
    small, one, two = call(order_body, (shape(block), shape(block), shape(block)))(
        *gather(small, from_ahead_x), top
    )
    pre_all = gather(call(join_body, shape((32, 4096)))(*messages), from_ahead_x)
    one, two = (swap(one, "slab", 1), swap_next(two))
    grad_act, second = call(
        second_body,
        (shape((128, 4096), f32), shape((4, 256, 128), f32)),
        (pltpu.VMEM((4, 256, 512), bf16), pltpu.VMEM((1024, 512), bf16)),
        micros=3.0,
    )(small, kernel_second, act, act_up)
    grad_halo, second, below = call(
        second_halo_body,
        (shape((128, 1024), f32), shape((256, 256)), shape((128, 1024))),
        (
            pltpu.VMEM((256, 1024), bf16),
            pltpu.VMEM((32, 1024), f32),
            pltpu.VMEM((128, 1024), f32),
        ),
        micros=2.0,
    )(one, two, kernel_second, act_up, second)
    grad_first, kept, sent = call(
        first_taps_body,
        (shape((128, 4096)), shape((8, 16, 384)), shape((8, 16, 384))),
        (pltpu.VMEM((128, 4096), f32), pltpu.VMEM((128, 128), f32)),
    )(*pre_all, grad_act, grad_halo, cols, below, second)
    edge = call(edge_body, shape((16, 1024)))(grad_first, kern)

    block = (2, 16, 384)
    kept, *sent = call(
        middle_body,
        (shape(block, f32), shape(block), shape(block), shape(block)),
        in_specs=[whole, whole, unread],
    )(kept, swap(sent, "slab", 1), edge)
    came = []
    for step in (1, 2, 3):
        pairs = [(s, (s & 9) | ((((s >> 1) + step) & 3) << 1)) for s in range(16)]
        came.append(lax.ppermute(sent[step - 1], "slab", pairs))
    kept, sent = call(late_body, (shape((16, 384), f32), shape((16, 384))))(kept, *came)
    grad_volume = call(first_body, shape((1, 4, 8, 4096)), (pltpu.VMEM((256, 512), f32),))(
        grad_first, kern, from_above(edge)
    )
    weight_first, weight_second = call(
        final_body, (shape((4, 8, 27), f32), shape((8, 16, 27), f32))
    )(kept, swap(sent, "slab", 8))
    return (
        grad_volume,
        jnp.transpose(weight_first, (2, 0, 1)),
        jnp.transpose(weight_second, (2, 0, 1)),
    )


def solution(mesh):
    return jax.shard_map(
        on_device,
        mesh=mesh,
        in_specs=(
            P(None, "chan", "slab", None),
            P(None, "chan", "slab", None),
            P(None, "chan", "slab", None),
            P(),
            P(),
            P(None, "chan", "slab", None),
            P(None, "chan", "slab", None),
        ),
        out_specs=(P(None, "chan", "slab", None), P(None, "chan", "slab"), P(None, "chan", "slab")),
        check_vma=False,
    )
```
